512 devices in a mesh: seq: 64 (over z, y_lo, x), head: 8 (over y_hi, core).
Axes of the slice: x: 4, y: 8 (y_hi: 4, y_lo: 2; y = y_hi * 2 + y_lo), z: 8, core: 2. Of those that a mesh axis runs over, the one named last changes fastest.
Arguments:
- queries: bfloat16 [65536, 4096], P(('seq', 'head')), may hold values from -5 to 5
- key_rows: bfloat16 [65536, 4096], P(('seq', 'head')), may hold values from -5 to 5
- value_rows: bfloat16 [65536, 4096], P(('seq', 'head')), may hold values from -6 to 6
- step_rates: bfloat16 [65536, 8], P(('seq', 'head')), may hold values from 0.1 to 9
- w_gate: bfloat16 [512, 8, 512], P('seq', 'head'), may hold values from -0.25 to 0.25
- w_up: bfloat16 [512, 8, 512], P('seq', 'head'), may hold values from -0.25 to 0.25
- w_down: bfloat16 [512, 8, 512], P('seq', 'head'), may hold values from -0.25 to 0.25
Outputs:
- block_out: bfloat16 [65536, 4096], P(('seq', 'head'))
The draws below stay inside these ranges and needn't reach their ends.
All inputs are finite; a program needn't handle non-finite values.
Results may differ from the reference program's by a relative error of at most 0.012.
Values may be sent and summed in bfloat16 or wider, within the bound.
A program may use at most 64 MiB of HBM per device.

```python
import math
import jax
import jax.numpy as jnp
from jax import lax

D = 4096
ATT_HEADS = 32
HEAD_DIM = 128
HEADS = 8
HS = 512
WINDOW = 64
TOKENS = 65536


def drawn_pair(key):
    rng_query = jax.random.fold_in(key, 11)
    rng_keys = jax.random.fold_in(key, 12)
    query_part = jnp.clip(jax.random.normal(rng_query, (TOKENS, D), jnp.float32), -5.0, 5.0)
    key_part = jnp.clip(jax.random.normal(rng_keys, (TOKENS, D), jnp.float32), -5.0, 5.0)
    return (query_part.astype(jnp.bfloat16), key_part.astype(jnp.bfloat16))


def draw_queries(key, part):
    return drawn_pair(key)[0]


def draw_key_rows(key, part):
    return drawn_pair(key)[1]


def draw_step_rates(key, part):
    position = jnp.arange(TOKENS, dtype=jnp.float32)[:, None] / TOKENS
    base_log = jax.random.uniform(jax.random.fold_in(key, 21), (TOKENS, HEADS), jnp.float32, jnp.log(0.1), 0.0)
    ramp_log = jnp.log(3.0) * position
    return jnp.exp(base_log + ramp_log).astype(jnp.bfloat16)


def level_of(rng, shape, shards, least, largest):
    def one(dim, blocks):
        steps = jax.random.uniform(jax.random.fold_in(jax.random.fold_in(rng, 6), dim), (blocks,), jnp.float32, least / len(shards), largest / len(shards))
        return jnp.repeat(jnp.exp(steps), shape[dim] // blocks).reshape((-1,) + (1,) * (len(shape) - dim - 1))

    factor_of = one(*shards[0])
    for cut in shards[1:]:
        factor_of = factor_of * one(*cut)
    return factor_of


def noise(own_key, shape, spread, limit, shards=(), kind=jnp.bfloat16):
    entries = jax.random.normal(own_key, shape, jnp.float32) * spread
    if len(shards) > 0:
        entries = level_of(own_key, shape, shards, -0.22, 0.18) * entries
    return jnp.clip(entries, min=-limit, max=limit).astype(kind)


def setup_inputs(seed: int = 0) -> dict:
    seeds = jax.random.split(jax.random.key(seed), 8)
    return {
        "queries": draw_queries(jax.random.fold_in(seeds[7], 71), 0),
        "key_rows": draw_key_rows(jax.random.fold_in(seeds[7], 71), 0),
        "value_rows": noise(seeds[2], (TOKENS, D), 1.0, 6.0, ((0, 512),)),
        "step_rates": draw_step_rates(jax.random.fold_in(seeds[7], 71), 0),
        "w_gate": noise(seeds[4], (HS, HEADS, HS), HS ** -0.5, 0.25, ((0, 64), (1, 8))),
        "w_up": noise(seeds[5], (HS, HEADS, HS), HS ** -0.5, 0.25, ((0, 64), (1, 8))),
        "w_down": noise(seeds[6], (HS, HEADS, HS), HS ** -0.5, 0.25, ((0, 64), (1, 8))),
    }


STEP_SIZE = 0.05
NORM_EPS = 1e-06
query_block = 512

def attend(block_queries, key_span, value_span, query_start):
    row_count = block_queries.shape[0]
    span_count = key_span.shape[0]
    query_heads = block_queries.astype(jnp.float32).reshape(row_count, ATT_HEADS, HEAD_DIM)
    key_heads = key_span.astype(jnp.float32).reshape(span_count, ATT_HEADS, HEAD_DIM)
    value_heads = value_span.astype(jnp.float32).reshape(span_count, ATT_HEADS, HEAD_DIM)
    scores = jnp.einsum('qhd,khd->hqk', query_heads, key_heads) * (1.0 / math.sqrt(HEAD_DIM))
    query_pos = query_start + jnp.arange(row_count, dtype=jnp.int32)
    key_pos = query_start - WINDOW + jnp.arange(span_count, dtype=jnp.int32)
    allowed = (key_pos[None, :] >= 0) & (key_pos[None, :] <= query_pos[:, None]) & (key_pos[None, :] > query_pos[:, None] - WINDOW)
    masked = jnp.where(allowed[None], scores, -1e+30)
    maximum = lax.optimization_barrier(jnp.max(masked, axis=2, keepdims=True))
    exp_scores = jnp.where(allowed[None], jnp.exp(masked - maximum), 0.0)
    totals = lax.optimization_barrier(jnp.sum(exp_scores, axis=2))
    weights = exp_scores.astype(jnp.bfloat16)
    mixed = jnp.einsum('hqk,khd->qhd', weights.astype(jnp.float32), value_heads)
    return (mixed / jnp.transpose(totals)[:, :, None]).reshape(row_count, D)

def rms_heads(tensor):
    blocks = tensor.astype(jnp.float32).reshape(tensor.shape[0], HEADS, HS)
    return (blocks * lax.rsqrt(lax.optimization_barrier(jnp.mean(blocks * blocks, axis=2, keepdims=True)) + NORM_EPS)).astype(jnp.bfloat16)

def renorm(old_rows, grad_rows, norm_scale):
    previous = old_rows.astype(jnp.float32)
    stepped = previous - STEP_SIZE * norm_scale * grad_rows
    factor = jnp.sqrt(lax.optimization_barrier(jnp.mean(previous * previous, axis=-1, keepdims=True))) * lax.rsqrt(lax.optimization_barrier(jnp.mean(stepped * stepped, axis=-1, keepdims=True)) + NORM_EPS)
    return (stepped * factor).astype(jnp.bfloat16)

def fast_head(inputs):
    key_norm, query_norm, value_head, rate_col, gate_w, up_w, down_w = inputs
    gate_pre = jnp.dot(key_norm, gate_w, preferred_element_type=jnp.float32)
    up_pre = jnp.dot(key_norm, up_w, preferred_element_type=jnp.float32)
    sigma_gate = jax.nn.sigmoid(gate_pre)
    silu_gate = gate_pre * sigma_gate
    hidden = (silu_gate * up_pre).astype(jnp.bfloat16)
    target = (-rate_col.astype(jnp.float32)[:, None] * value_head.astype(jnp.float32)).astype(jnp.bfloat16)
    hidden_grad = jnp.dot(target, jnp.transpose(down_w), preferred_element_type=jnp.float32)
    gate_grad = (hidden_grad * up_pre * sigma_gate * (1.0 + gate_pre * (1.0 - sigma_gate))).astype(jnp.bfloat16)
    up_grad = (hidden_grad * silu_gate).astype(jnp.bfloat16)
    sum_gate = jnp.dot(jnp.transpose(key_norm), gate_grad, preferred_element_type=jnp.float32)
    sum_up = jnp.dot(jnp.transpose(key_norm), up_grad, preferred_element_type=jnp.float32)
    sum_down = jnp.dot(jnp.transpose(hidden), target, preferred_element_type=jnp.float32)
    squares = jnp.sum(sum_gate * sum_gate) + jnp.sum(sum_up * sum_up) + jnp.sum(sum_down * sum_down)
    norm_scale = lax.rsqrt(squares / (3 * HS * HS) + NORM_EPS)
    new_gate = renorm(gate_w, sum_gate, norm_scale)
    new_up = renorm(up_w, sum_up, norm_scale)
    new_down = renorm(down_w, sum_down, norm_scale)
    query_gate = jnp.dot(query_norm, new_gate, preferred_element_type=jnp.float32)
    query_up = jnp.dot(query_norm, new_up, preferred_element_type=jnp.float32)
    query_hidden = (query_gate * jax.nn.sigmoid(query_gate) * query_up).astype(jnp.bfloat16)
    return jnp.dot(query_hidden, new_down, preferred_element_type=jnp.float32).astype(jnp.bfloat16)

def reference(queries, key_rows, value_rows, step_rates, w_gate, w_up, w_down):
    block_rows = min(query_block, TOKENS)
    padded_keys = jnp.concatenate([jnp.zeros((WINDOW, D), key_rows.dtype), key_rows], 0)
    padded_values = jnp.concatenate([jnp.zeros((WINDOW, D), value_rows.dtype), value_rows], 0)
    starts = jnp.arange(TOKENS // block_rows, dtype=jnp.int32) * block_rows

    def one_block(begin_row):
        block_queries = lax.dynamic_slice_in_dim(queries, begin_row, block_rows, 0)
        key_span = lax.dynamic_slice_in_dim(padded_keys, begin_row, block_rows + WINDOW, 0)
        value_span = lax.dynamic_slice_in_dim(padded_values, begin_row, block_rows + WINDOW, 0)
        return attend(block_queries, key_span, value_span, begin_row)
    attended = lax.map(one_block, starts).reshape(TOKENS, D)
    key_norm = rms_heads(key_rows)
    query_norm = rms_heads(queries)
    value_heads = value_rows.reshape(TOKENS, HEADS, HS)
    per_head = (jnp.transpose(key_norm, (1, 0, 2)), jnp.transpose(query_norm, (1, 0, 2)), jnp.transpose(value_heads, (1, 0, 2)), jnp.transpose(step_rates), jnp.transpose(w_gate, (1, 0, 2)), jnp.transpose(w_up, (1, 0, 2)), jnp.transpose(w_down, (1, 0, 2)))
    fast_out = lax.map(fast_head, per_head)
    merged = jnp.transpose(fast_out, (1, 0, 2)).reshape(TOKENS, D)
    return (attended + merged.astype(jnp.float32)).astype(jnp.bfloat16)
```

```python
import math

import jax
import jax.numpy as jnp
from jax import lax
from jax.experimental import pallas as pl
from jax.experimental.pallas import tpu as pltpu
from jax.sharding import Mesh
from jax.sharding import PartitionSpec as P

HEAD_DIM = 128
HEADS = 8
HS = 512
WINDOW = 64
STEP_SIZE = 0.05
NORM_EPS = 1e-06
ROWS = 128
D = HEADS * HS
NX, NY, NZ = 4, 8, 8
AXES = ("z", "yl", "x", "yh", "c")
MESH = pl.DeviceIdType.MESH
F32, BF16 = jnp.float32, jnp.bfloat16
WAYS = ((1, 0, 1, 0), (7, 0, -1, 0), (3, 0, 0, 1), (5, 0, 0, -1), (2, 1, 0, 0), (6, -1, 0, 0), (4, 0, 1, 1))
OWN = len(WAYS)


def fast_kernel(
    q_hbm, k_hbm, v_hbm, rate_ref, w_ref, out_ref,
    ql, kl, vl, tl, halo, kb, vb, qb, wrecv, wfull, gu, hid, gown, gsend, gex, gb, rsb, agb, wnew, fo, ret, att,
    lsem, wsend, wrecv_sem, wfsend, wfrecv, ksend, krecv, vsend, vrecv, qsend, qrecv, hsend, hrecv,
    exsend, exrecv, rssend, rsrecv, agsend, agrecv, agfsend, agfrecv, osend, orecv,
):
    z, yl, x, yh, c = (lax.axis_index(a) for a in AXES)
    y = 2 * yh + yl
    colour = lax.rem(2 * x + y + 3 * z, 8)
    sign = 1 - 2 * c
    other = (z, yl, x, yh, 1 - c)
    spot = z * NX + x

    def device(px, py, pz, core):
        py = lax.rem(py + 64, NY)
        return (lax.rem(pz + 64, NZ), lax.rem(py, 2), lax.rem(px + 64, NX), py // 2, core)

    def there(way, back=1):
        _, dx, dy, dz = WAYS[way]
        turn = sign if way == OWN - 1 else 1
        return device(x + back * dx, y + back * turn * dy, z + back * turn * dz, c)

    def head_of(way):
        return colour if way == OWN else lax.rem(colour + WAYS[way][0], 8)

    def remote(src, dst, send, recv, dev):
        return pltpu.make_async_remote_copy(
            src_ref=src, dst_ref=dst, send_sem=send, recv_sem=recv, device_id=dev, device_id_type=MESH
        )

    def columns(head):
        return pl.ds(pl.multiple_of(head * HS, HS), HS)

    loads = [pltpu.make_async_copy(v_hbm, vl, lsem.at[0]), pltpu.make_async_copy(k_hbm, kl, lsem.at[1]),
             pltpu.make_async_copy(q_hbm, ql, lsem.at[2])]
    for load in loads:
        load.start()
    for way in range(OWN):
        remote(k_hbm.at[:, columns(head_of(way))], kb.at[way], ksend, krecv.at[way], there(way)).start()

    my_head = 2 * yh + c
    is_self = (my_head == colour) & (yl == c)

    def weight_dest(dx, dz):
        px, pz = x + dx, z + dz
        return device(px, my_head - 2 * px - 3 * pz, pz, yl)

    @pl.when(is_self)
    def _():
        wrecv[yl, spot] = w_ref[...]

    @pl.when(jnp.logical_not(is_self))
    def _():
        remote(w_ref, wrecv.at[yl, spot], wsend, wrecv_sem.at[0], weight_dest(0, 0)).start()

    def send_weights(i, carry):
        dx, dz = lax.rem(i, NX), i // NX
        remote(w_ref, wrecv.at[yl, spot], wsend, wrecv_sem.at[dz], weight_dest(dx, dz)).start()
        return carry

    lax.fori_loop(1, NX * NZ, send_weights, 0)

    loads[0].wait()
    for head in range(HEADS):
        rate = rate_ref[:, head : head + 1].astype(F32)
        tl[head] = (-rate * vl[:, head * HS : (head + 1) * HS].astype(F32)).astype(BF16)
    for way in range(OWN):
        remote(tl.at[head_of(way)], vb.at[way], vsend, vrecv.at[way], there(way)).start()
    vb[OWN] = tl[colour]
    loads[1].wait()
    kb[OWN] = kl[:, columns(colour)]

    def unpack(half, pz):
        for pair in range(NX // 2):
            one = wrecv[half, pz * NX + 2 * pair].astype(F32)
            two = wrecv[half, pz * NX + 2 * pair + 1].astype(F32)
            rows = pl.ds(pl.multiple_of(((pz * 2 + half) * NX + 2 * pair) * 8, 16), 16)
            wfull[rows, : 3 * HS // 2] = jnp.concatenate([one[:8], two[:8]], 0).astype(BF16)
            wfull[rows, 3 * HS // 2 :] = jnp.concatenate([one[8:], two[8:]], 0).astype(BF16)

    def weights_in(dz, carry):
        pz = lax.rem(z - dz + NZ, NZ)

        @pl.when(is_self & (dz == 0))
        def _():
            part = wrecv.at[c, pl.ds(0, NX - 1)]
            remote(part, part, wsend, wrecv_sem.at[dz], other).wait_recv()

        @pl.when(jnp.logical_not(is_self & (dz == 0)))
        def _():
            part = wrecv.at[c, pl.ds(0, NX)]
            remote(part, part, wsend, wrecv_sem.at[dz], other).wait_recv()

        part = wrecv.at[c, pl.ds(pz * NX, NX)]
        remote(part, part, wfsend, wfrecv, other).start()
        unpack(c, pz)
        return carry

    lax.fori_loop(0, NZ, weights_in, 0)

    def normed(block):
        wide = block.astype(F32)
        return (wide * lax.rsqrt(jnp.mean(wide * wide, axis=-1, keepdims=True) + NORM_EPS)).astype(BF16)

    for way in range(OWN + 1):
        if way < OWN:
            remote(kb.at[way], kb.at[way], ksend, krecv.at[way], other).wait_recv()
        kb[way] = normed(kb[way])

    remote(wrecv.at[1 - c], wrecv.at[1 - c], wfsend, wfrecv, other).wait_recv()

    def unpack_other(pz, carry):
        unpack(1 - c, pz)
        return carry

    lax.fori_loop(0, NZ, unpack_other, 0)

    for way in range(OWN):
        remote(vb.at[way], vb.at[way], vsend, vrecv.at[way], other).wait_recv()

    for way in range(OWN):
        remote(q_hbm.at[:, columns(head_of(way))], qb.at[way], qsend, qrecv.at[way], there(way)).start()
    place = (((z * 2 + yl) * NX + x) * 4 + yh) * 2 + c
    after = lax.rem(place + 1, 512)
    next_block = (after // 64, lax.rem(after // 32, 2), lax.rem(after // 8, 4), lax.rem(after // 2, 4), lax.rem(after, 2))
    remote(kl.at[pl.ds(ROWS - WINDOW, WINDOW)], halo.at[0], hsend, hrecv, next_block).start()
    remote(vl.at[pl.ds(ROWS - WINDOW, WINDOW)], halo.at[1], hsend, hrecv, next_block).start()
    loads[2].wait()
    qb[OWN] = normed(ql[:, columns(colour)])

    def tokens(i, carry):
        keys = kb[pl.ds(2 * i, 2)].reshape(2 * ROWS, HS)
        target = vb[pl.ds(2 * i, 2)].reshape(2 * ROWS, HS)
        gate_pre = jnp.dot(keys, wfull[:, :HS], preferred_element_type=F32)
        up_pre = jnp.dot(keys, wfull[:, HS : 2 * HS], preferred_element_type=F32)
        hidden_grad = lax.dot_general(
            target, wfull[:, 2 * HS :], (((1,), (1,)), ((), ())), preferred_element_type=F32
        )
        sigma = jax.nn.sigmoid(gate_pre)
        silu = gate_pre * sigma
        hid[pl.ds(2 * i, 2)] = (silu * up_pre).astype(BF16).reshape(2, ROWS, HS)
        gate_grad = (hidden_grad * up_pre * sigma * (1.0 + gate_pre * (1.0 - sigma))).astype(BF16)
        up_grad = (hidden_grad * silu).astype(BF16)
        for half in range(2):
            part = slice(half * HS // 2, (half + 1) * HS // 2)
            gu[half, pl.ds(2 * i, 2), :, : HS // 2] = gate_grad[:, part].reshape(2, ROWS, HS // 2)
            gu[half, pl.ds(2 * i, 2), :, HS // 2 :] = up_grad[:, part].reshape(2, ROWS, HS // 2)
        return carry

    lax.fori_loop(0, 4, tokens, 0)

    def half_sums(half, store):
        def rows(i, carry):
            span = pl.ds(pl.multiple_of(i * 256, 256), 256)
            keys = kb[:, :, span].reshape(8 * ROWS, 256)
            grads = gu[half].reshape(8 * ROWS, HS)
            hidden = hid[:, :, span].reshape(8 * ROWS, 256)
            target = vb[:, :, pl.ds(pl.multiple_of(half * 256, 256), 256)].reshape(8 * ROWS, 256)
            over_tokens = (((0,), (0,)), ((), ()))
            store[span, :HS] = lax.dot_general(keys, grads, over_tokens, preferred_element_type=F32).astype(store.dtype)
            store[span, HS:] = lax.dot_general(hidden, target, over_tokens, preferred_element_type=F32).astype(store.dtype)
            return carry

        lax.fori_loop(0, 2, rows, 0)

    half_sums(1 - c, gsend)
    exchange = remote(gsend, gex, exsend, exrecv, other)
    exchange.start()
    half_sums(c, gown)
    exchange.wait_recv()

    def mate(dx, dz):
        return device(x + dx, y - 2 * dx - 3 * dz, z + dz, c)

    def send_sums(dz, carry):
        pz = lax.rem(z + dz, NZ)
        rows = pl.ds(pl.multiple_of(pz * 64, 64), 64)
        gb[pl.ds(pz * NX, NX)] = (gown[rows, :] + gex[rows, :].astype(F32)).astype(BF16).reshape(NX, 16, 3 * HS // 2)
        for dx in range(NX):
            px = lax.rem(x + dx, NX)

            def go():
                remote(gb.at[pz * NX + px], rsb.at[spot], rssend, rsrecv, mate(dx, dz)).start()

            if dx == 0:
                pl.when(dz > 0)(go)
            else:
                go()
        return carry

    lax.fori_loop(0, NZ, send_sums, 0)
    rsb[spot] = gb[spot]

    remote(halo, halo, hsend, hrecv, other).wait_recv()
    span_rows = ROWS + WINDOW
    at_row = lax.broadcasted_iota(jnp.int32, (ROWS, span_rows), 0)
    at_key = lax.broadcasted_iota(jnp.int32, (ROWS, span_rows), 1)
    allowed = (at_key > at_row) & (at_key <= at_row + WINDOW) & (at_key + place * ROWS >= WINDOW)

    def attend(head, carry):
        cols = columns(head)
        queries = ql[:, cols]
        keys = jnp.concatenate([halo[0, :, cols], kl[:, cols]], 0)
        values = jnp.concatenate([halo[1, :, cols], vl[:, cols]], 0)
        for sub in range(HS // HEAD_DIM):
            part = slice(sub * HEAD_DIM, (sub + 1) * HEAD_DIM)
            scores = lax.dot_general(
                queries[:, part], keys[:, part], (((1,), (1,)), ((), ())), preferred_element_type=F32
            ) * (1.0 / math.sqrt(HEAD_DIM))
            masked = jnp.where(allowed, scores, -1e30)
            maximum = jnp.max(masked, axis=1, keepdims=True)
            weights = jnp.where(allowed, jnp.exp(masked - maximum), 0.0)
            totals = jnp.sum(weights, axis=1, keepdims=True)
            mixed = jnp.dot(weights.astype(BF16), values[:, part], preferred_element_type=F32)
            att[head, :, part] = mixed / totals
        return carry

    lax.fori_loop(0, HEADS, attend, 0)

    for way in range(OWN):
        remote(qb.at[way], qb.at[way], qsend, qrecv.at[way], other).wait_recv()
        qb[way] = normed(qb[way])

    others = rsb.at[pl.ds(0, NX * NZ - 1)]
    remote(others, others, rssend, rsrecv, other).wait_recv()

    def add_up(i, total):
        return total + jnp.sum(rsb[pl.ds(i * NX, NX)].astype(F32), axis=0)

    agb[c, spot] = lax.fori_loop(0, NZ, add_up, jnp.zeros((16, 3 * HS // 2), F32)).astype(BF16)

    def spread(i, carry):
        dx, dz = lax.rem(i, NX), i // NX
        remote(agb.at[c, spot], agb.at[c, spot], agsend, agrecv.at[dz], mate(dx, dz)).start()
        return carry

    lax.fori_loop(1, NX * NZ, spread, 0)

    def sums_in(dz, carry):
        pz = lax.rem(z - dz + NZ, NZ)

        @pl.when(dz == 0)
        def _():
            part = agb.at[c, pl.ds(0, NX - 1)]
            remote(part, part, agsend, agrecv.at[dz], other).wait_recv()

        @pl.when(dz > 0)
        def _():
            part = agb.at[c, pl.ds(0, NX)]
            remote(part, part, agsend, agrecv.at[dz], other).wait_recv()

        part = agb.at[c, pl.ds(pz * NX, NX)]
        remote(part, part, agfsend, agfrecv, other).start()
        return carry

    lax.fori_loop(0, NZ, sums_in, 0)
    remote(agb.at[1 - c], agb.at[1 - c], agfsend, agfrecv, other).wait_recv()

    def squares(i, total):
        for half in range(2):
            part = agb[half, pl.ds(i * NX, NX)].astype(F32).reshape(64, 3 * HS // 2)
            total = total + jnp.sum(part * part, axis=0, keepdims=True)
        return total

    square_sum = jnp.sum(lax.fori_loop(0, NZ, squares, jnp.zeros((1, 3 * HS // 2), F32)), axis=1, keepdims=True)
    step = STEP_SIZE * lax.rsqrt(square_sum * (1.0 / (3 * HS * HS)) + NORM_EPS)

    def renorm(i, carry):
        rows = pl.ds(pl.multiple_of(i * 64, 64), 64)
        low = agb[0, pl.ds(i * NX, NX)].astype(F32).reshape(64, 3 * HS // 2)
        high = agb[1, pl.ds(i * NX, NX)].astype(F32).reshape(64, 3 * HS // 2)
        for which in range(3):
            part = slice(which * HS // 2, (which + 1) * HS // 2)
            grads = jnp.concatenate([low[:, part], high[:, part]], 1)
            previous = wfull[rows, which * HS : (which + 1) * HS].astype(F32)
            stepped = previous - step * grads
            factor = jnp.sqrt(jnp.mean(previous * previous, axis=-1, keepdims=True)) * lax.rsqrt(
                jnp.mean(stepped * stepped, axis=-1, keepdims=True) + NORM_EPS
            )
            wnew[rows, which * HS : (which + 1) * HS] = (stepped * factor).astype(BF16)
        return carry

    lax.fori_loop(0, NZ, renorm, 0)

    for pair in range(4):
        queries = qb[2 * pair : 2 * pair + 2].reshape(2 * ROWS, HS)
        gate = jnp.dot(queries, wnew[:, :HS], preferred_element_type=F32)
        up = jnp.dot(queries, wnew[:, HS : 2 * HS], preferred_element_type=F32)
        hidden = (gate * jax.nn.sigmoid(gate) * up).astype(BF16)
        result = jnp.dot(hidden, wnew[:, 2 * HS :], preferred_element_type=F32)
        fo[2 * pair : 2 * pair + 2] = result.astype(BF16).reshape(2, ROWS, HS)
        for way in (2 * pair, 2 * pair + 1):
            if way < OWN:
                remote(fo.at[way], ret.at[way], osend, orecv.at[way], there(way, -1)).start()
    ret[OWN] = fo[OWN]
    for way in (OWN, *range(OWN)):
        if way < OWN:
            remote(ret.at[way], ret.at[way], osend, orecv.at[way], other).wait_recv()
        head = head_of(way)
        out_ref[:, columns(head)] = (att[head] + ret[way].astype(F32)).astype(BF16)

    for buffer, sem in ((kb, ksend), (vb, vsend), (qb, qsend), (ret, osend)):
        sent = buffer.at[pl.ds(0, OWN)]
        remote(sent, sent, sem, orecv.at[0], other).wait_send()
    remote(halo, halo, hsend, hrecv, other).wait_send()
    exchange.wait_send()
    for buffer, sem in ((rsb, rssend), (agb.at[0], agsend)):
        sent = buffer.at[pl.ds(0, NX * NZ - 1)]
        remote(sent, sent, sem, orecv.at[0], other).wait_send()

    @pl.when(is_self)
    def _():
        sent = wrecv.at[0, pl.ds(0, NX * NZ - 1)]
        remote(sent, sent, wsend, orecv.at[0], other).wait_send()

    @pl.when(jnp.logical_not(is_self))
    def _():
        remote(wrecv.at[0], wrecv.at[0], wsend, orecv.at[0], other).wait_send()

    for buffer, sem in ((wrecv.at[0], wfsend), (agb.at[0], agfsend)):
        remote(buffer, buffer, sem, orecv.at[0], other).wait_send()


def shards(queries, key_rows, value_rows, step_rates, w_gate, w_up, w_down):
    own = jnp.concatenate([w_gate, w_up, w_down], 2).reshape(8, 3 * HS)
    own = jnp.concatenate([own[:, : 3 * HS // 2], own[:, 3 * HS // 2 :]], 0)
    hbm = pl.BlockSpec(memory_space=pl.ANY)
    vmem = pl.BlockSpec(memory_space=pltpu.VMEM)
    wide = 3 * HS // 2
    blocks = pltpu.VMEM((8, ROWS, HS), BF16)
    dma = pltpu.SemaphoreType.DMA
    return pl.pallas_call(
        fast_kernel,
        out_shape=jax.ShapeDtypeStruct((ROWS, D), BF16),
        in_specs=[hbm, hbm, hbm, vmem, vmem],
        out_specs=vmem,
        scratch_shapes=[
            pltpu.VMEM((ROWS, D), BF16),
            pltpu.VMEM((ROWS, D), BF16),
            pltpu.VMEM((ROWS, D), BF16),
            blocks,
            pltpu.VMEM((2, WINDOW, D), BF16),
            blocks,
            blocks,
            blocks,
            pltpu.VMEM((2, NZ * NX, 16, wide), BF16),
            pltpu.VMEM((HS, 3 * HS), BF16),
            pltpu.VMEM((2, 8, ROWS, HS), BF16),
            blocks,
            pltpu.VMEM((HS, wide), F32),
            pltpu.VMEM((HS, wide), BF16),
            pltpu.VMEM((HS, wide), BF16),
            pltpu.VMEM((NZ * NX, 16, wide), BF16),
            pltpu.VMEM((NZ * NX, 16, wide), BF16),
            pltpu.VMEM((2, NZ * NX, 16, wide), BF16),
            pltpu.VMEM((HS, 3 * HS), BF16),
            blocks,
            blocks,
            pltpu.VMEM((8, ROWS, HS), F32),
            dma((3,)),
            dma, dma((NZ,)), dma, dma,
            dma, dma((OWN,)), dma, dma((OWN,)), dma, dma((OWN,)),
            dma, dma,
            dma, dma,
            dma, dma,
            dma, dma((NZ,)), dma, dma,
            dma, dma((OWN,)),
        ],
        compiler_params=pltpu.CompilerParams(has_side_effects=True, vmem_limit_bytes=56 * 1024 * 1024),
    )(queries, key_rows, value_rows, step_rates, own)


def solution(mesh):
    torus = Mesh(mesh.devices.reshape(NZ, 2, NX, 4, 2), AXES)
    seq = ("z", "yl", "x")
    head = ("yh", "c")
    return jax.shard_map(
        shards,
        mesh=torus,
        in_specs=(
            P((*seq, *head), None),
            P((*seq, *head), None),
            P((*seq, *head), None),
            P((*seq, *head), None),
            P(seq, head, None),
            P(seq, head, None),
            P(seq, head, None),
        ),
        out_specs=P((*seq, *head), None),
        check_vma=False,
    )
```

```python
import math

import jax
import jax.numpy as jnp
from jax import lax
from jax.experimental import pallas as pl
from jax.experimental.pallas import tpu as pltpu
from jax.sharding import Mesh
from jax.sharding import PartitionSpec as P

HEAD_DIM = 128
HEADS = 8
HS = 512
WINDOW = 64
STEP_SIZE = 0.05
NORM_EPS = 1e-06
ROWS = 128
D = HEADS * HS
NX, NY, NZ = 4, 8, 8
AXES = ("z", "yl", "x", "yh", "c")
MESH = pl.DeviceIdType.MESH
F32, BF16 = jnp.float32, jnp.bfloat16
WAYS = ((1, 0, 1, 0), (7, 0, -1, 0), (3, 0, 0, 1), (5, 0, 0, -1), (2, 1, 0, 0), (6, -1, 0, 0), (4, 0, 1, 1))
OWN = len(WAYS)


def fast_kernel(
    q_hbm, k_hbm, v_hbm, rate_ref, wg_ref, wu_ref, wd_ref, out_ref,
    ql, kl, vl, tl, halo, kb, vb, qb, wpack, wrecv, wfull, gu, hid, gown, gsend, gex, gb, near, part_sum, far, agb, wnew, fo, ret, att,
    lsem, wcsend, wcrecv, wtsend, wtrecv, wssend, wsrecv, wfsend, wfrecv, ksend, krecv, vsend, vrecv, qsend, qrecv,
    hsend, hrecv, exsend, exrecv, nsend, nrecv, fsend, frecv, atsend, atrecv, assend, asrecv, afsend, afrecv, osend, orecv,
):
    z, yl, x, yh, c = (lax.axis_index(a) for a in AXES)
    y = 2 * yh + yl
    colour = lax.rem(2 * x + y + 3 * z, 8)
    sign = 1 - 2 * c
    other = (z, yl, x, yh, 1 - c)
    skew = 2 * (1 - c)
    line = lax.rem(z - skew * x + 64, NZ)
    spot = line * NX + x
    place = (((z * 2 + yl) * NX + x) * 4 + yh) * 2 + c

    def device(px, py, pz, core):
        py = lax.rem(py + 64, NY)
        return (lax.rem(pz + 64, NZ), lax.rem(py, 2), lax.rem(px + 64, NX), py // 2, core)

    def there(way, back=1):
        _, dx, dy, dz = WAYS[way]
        turn = sign if way == OWN - 1 else 1
        return device(x + back * dx, y + back * turn * dy, z + back * turn * dz, c)

    def head_of(way):
        return colour if way == OWN else lax.rem(colour + WAYS[way][0], 8)

    def remote(src, dst, send, recv, dev):
        return pltpu.make_async_remote_copy(
            src_ref=src, dst_ref=dst, send_sem=send, recv_sem=recv, device_id=dev, device_id_type=MESH
        )

    def columns(head):
        return pl.ds(pl.multiple_of(head * HS, HS), HS)

    def near_mate(step):
        dz = skew * step
        return device(x + step, y - 2 * step - 3 * dz, z + dz, c)

    def far_mate(step):
        return device(x, y - 3 * step, z + step, c)

    def block_at(index):
        index = lax.rem(index + 512, 512)
        return (index // 64, lax.rem(index // 32, 2), lax.rem(index // 8, 4), lax.rem(index // 2, 4), lax.rem(index, 2))

    my_head = 2 * yh + c
    is_self = (my_head == colour) & (yl == c)
    weight_dest = device(x, my_head - 2 * x - 3 * z, z, yl)
    weight_source = (z, c, x, colour // 2, lax.rem(colour, 2))

    barrier = pltpu.get_barrier_semaphore()
    partners = [there(way) for way in range(OWN)] + [there(OWN - 1, -1), other, block_at(place + 1), block_at(place - 1)]
    partners += [near_mate(step) for step in range(1, NX)] + [far_mate(step) for step in range(1, NZ)]

    def greet(dev):
        pl.semaphore_signal(barrier, inc=1, device_id=dev, device_id_type=MESH)

    for dev in partners:
        greet(dev)

    @pl.when(jnp.logical_not(is_self))
    def _():
        greet(weight_dest)
        greet(weight_source)

    loads = [pltpu.make_async_copy(v_hbm, vl, lsem.at[0]), pltpu.make_async_copy(k_hbm, kl, lsem.at[1]),
             pltpu.make_async_copy(q_hbm, ql, lsem.at[2])]
    for load in loads:
        load.start()
    gate_rows, up_rows, down_rows = (ref[...].astype(F32) for ref in (wg_ref, wu_ref, wd_ref))
    wpack[...] = jnp.concatenate(
        [jnp.concatenate([gate_rows, up_rows[:, : HS // 2]], 1), jnp.concatenate([up_rows[:, HS // 2 :], down_rows], 1)], 0
    ).astype(BF16)

    @pl.when(is_self)
    def _():
        pl.semaphore_wait(barrier, len(partners))

    @pl.when(jnp.logical_not(is_self))
    def _():
        pl.semaphore_wait(barrier, len(partners) + 2)

    dest_spot = lax.rem(z - 2 * (1 - yl) * x + 64, NZ) * NX + x

    @pl.when(is_self)
    def _():
        wrecv[yl, dest_spot] = wpack[...]

    @pl.when(jnp.logical_not(is_self))
    def _():
        remote(wpack, wrecv.at[yl, dest_spot], wcsend, wcrecv, weight_dest).start()

    for way in range(OWN):
        remote(k_hbm.at[:, columns(head_of(way))], kb.at[way], ksend, krecv.at[way], there(way)).start()

    def far_sends(buffer, send, recv):
        def go(step, carry):
            block = buffer.at[c, spot]
            remote(block, block, send, recv.at[step], far_mate(step)).start()
            return carry

        lax.fori_loop(1, NZ, go, 0)

    def near_sends(buffer, send, recv, nsend_, nrecv_):
        def go(step, carry):
            block = buffer.at[c, lax.rem(line - step + NZ, NZ) * NX + x]

            @pl.when(step > 0)
            def _():
                remote(block, block, send, recv.at[step], other).wait_recv()

            for move in range(1, NX):
                remote(block, block, nsend_, nrecv_.at[step], near_mate(move)).start()
            return carry

        lax.fori_loop(0, NZ, go, 0)

    def cross_sends(buffer, nsend_, nrecv_, csend, crecv, beside=None):
        def go(step, carry):
            if beside is not None:
                beside(step, 0)
            three = buffer.at[c, pl.ds(0, NX - 1)]
            remote(three, three, nsend_, nrecv_.at[step], other).wait_recv()
            four = buffer.at[c, pl.ds(lax.rem(line - step + NZ, NZ) * NX, NX)]
            remote(four, four, csend, crecv, other).start()
            return carry

        lax.fori_loop(0, NZ, go, 0)

    def crossed(buffer, csend, crecv):
        remote(buffer.at[1 - c], buffer.at[1 - c], csend, crecv, other).wait_recv()

    @pl.when(jnp.logical_not(is_self))
    def _():
        remote(wpack, wpack, wcsend, wcrecv, other).wait_recv()

    far_sends(wrecv, wtsend, wtrecv)
    rates = jnp.transpose(rate_ref[...].astype(F32))
    loads[0].wait()
    for head in range(HEADS):
        rate = rates[:, head : head + 1]
        tl[head] = (-rate * vl[:, head * HS : (head + 1) * HS].astype(F32)).astype(BF16)
    for way in range(OWN):
        remote(tl.at[head_of(way)], vb.at[way], vsend, vrecv.at[way], there(way)).start()
    vb[OWN] = tl[colour]
    loads[1].wait()
    kb[OWN] = kl[:, columns(colour)]

    near_sends(wrecv, wtsend, wtrecv, wssend, wsrecv)

    def unpack(half):
        def rows_of(pz, carry):
            for px in range(0, NX, 2):
                one, two = (
                    wrecv[half, lax.rem(pz - 2 * (1 - half) * at + 64, NZ) * NX + at].astype(F32) for at in (px, px + 1)
                )
                rows = pl.ds(pl.multiple_of(((pz * 2 + half) * NX + px) * 8, 16), 16)
                wfull[rows, : 3 * HS // 2] = jnp.concatenate([one[:8], two[:8]], 0).astype(BF16)
                wfull[rows, 3 * HS // 2 :] = jnp.concatenate([one[8:], two[8:]], 0).astype(BF16)
            return carry

        lax.fori_loop(0, NZ, rows_of, 0)

    def normed(block):
        wide = block.astype(F32)
        return (wide * lax.rsqrt(jnp.mean(wide * wide, axis=-1, keepdims=True) + NORM_EPS)).astype(BF16)

    for way in range(OWN + 1):
        if way < OWN:
            remote(kb.at[way], kb.at[way], ksend, krecv.at[way], other).wait_recv()
        kb[way] = normed(kb[way])

    cross_sends(wrecv, wssend, wsrecv, wfsend, wfrecv)
    unpack(c)
    crossed(wrecv, wfsend, wfrecv)
    unpack(1 - c)

    for way in range(OWN):
        remote(vb.at[way], vb.at[way], vsend, vrecv.at[way], other).wait_recv()

    for way in range(OWN):
        remote(q_hbm.at[:, columns(head_of(way))], qb.at[way], qsend, qrecv.at[way], there(way)).start()
    next_block = block_at(place + 1)
    remote(kl.at[pl.ds(ROWS - WINDOW, WINDOW)], halo.at[0], hsend, hrecv, next_block).start()
    remote(vl.at[pl.ds(ROWS - WINDOW, WINDOW)], halo.at[1], hsend, hrecv, next_block).start()
    loads[2].wait()
    qb[OWN] = normed(ql[:, columns(colour)])

    def tokens(i, carry):
        keys = kb[pl.ds(2 * i, 2)].reshape(2 * ROWS, HS)
        target = vb[pl.ds(2 * i, 2)].reshape(2 * ROWS, HS)
        gate_pre = jnp.dot(keys, wfull[:, :HS], preferred_element_type=F32)
        up_pre = jnp.dot(keys, wfull[:, HS : 2 * HS], preferred_element_type=F32)
        hidden_grad = lax.dot_general(
            target, wfull[:, 2 * HS :], (((1,), (1,)), ((), ())), preferred_element_type=F32
        )
        sigma = jax.nn.sigmoid(gate_pre)
        silu = gate_pre * sigma
        hid[pl.ds(2 * i, 2)] = (silu * up_pre).astype(BF16).reshape(2, ROWS, HS)
        gate_grad = (hidden_grad * up_pre * sigma * (1.0 + gate_pre * (1.0 - sigma))).astype(BF16)
        up_grad = (hidden_grad * silu).astype(BF16)
        for half in range(2):
            part = slice(half * HS // 2, (half + 1) * HS // 2)
            gu[half, pl.ds(2 * i, 2), :, : HS // 2] = gate_grad[:, part].reshape(2, ROWS, HS // 2)
            gu[half, pl.ds(2 * i, 2), :, HS // 2 :] = up_grad[:, part].reshape(2, ROWS, HS // 2)
        return carry

    lax.fori_loop(0, 4, tokens, 0)

    def half_sums(half, store):
        def rows(i, carry):
            span = pl.ds(pl.multiple_of(i * 256, 256), 256)
            keys = kb[:, :, span].reshape(8 * ROWS, 256)
            grads = gu[half].reshape(8 * ROWS, HS)
            hidden = hid[:, :, span].reshape(8 * ROWS, 256)
            target = vb[:, :, pl.ds(pl.multiple_of(half * 256, 256), 256)].reshape(8 * ROWS, 256)
            over_tokens = (((0,), (0,)), ((), ()))
            store[span, :HS] = lax.dot_general(keys, grads, over_tokens, preferred_element_type=F32).astype(store.dtype)
            store[span, HS:] = lax.dot_general(hidden, target, over_tokens, preferred_element_type=F32).astype(store.dtype)
            return carry

        lax.fori_loop(0, 2, rows, 0)

    half_sums(1 - c, gsend)
    exchange = remote(gsend, gex, exsend, exrecv, other)
    exchange.start()
    half_sums(c, gown)
    exchange.wait_recv()

    def near_sums(i, carry):
        step = lax.rem(i + 1, NZ)
        to = lax.rem(line + step, NZ)
        rows = pl.ds(pl.multiple_of(to * 64, 64), 64)
        gb[pl.ds(to * NX, NX)] = (gown[rows, :] + gex[rows, :].astype(F32)).astype(BF16).reshape(NX, 16, 3 * HS // 2)
        for move in range(1, NX):
            block = gb.at[to * NX + lax.rem(x + move, NX)]
            remote(block, near.at[to * NX + x], nsend, nrecv.at[step], near_mate(move)).start()
        return carry

    lax.fori_loop(0, NZ, near_sums, 0)

    for way in range(OWN):
        remote(qb.at[way], qb.at[way], qsend, qrecv.at[way], other).wait_recv()
        qb[way] = normed(qb[way])

    def far_sums(i, carry):
        step = lax.rem(i + 1, NZ)
        to = lax.rem(line + step, NZ)
        three = near.at[pl.ds(0, NX - 1)]
        remote(three, three, nsend, nrecv.at[step], other).wait_recv()
        near[to * NX + x] = gb[to * NX + x]
        part_sum[to] = jnp.sum(near[pl.ds(to * NX, NX)].astype(F32), axis=0).astype(BF16)

        @pl.when(step > 0)
        def _():
            remote(part_sum.at[to], far.at[line], fsend, frecv, far_mate(step)).start()

        return carry

    lax.fori_loop(0, NZ, far_sums, 0)
    far[line] = part_sum[line]

    span_rows = ROWS + WINDOW
    at_row = lax.broadcasted_iota(jnp.int32, (ROWS, span_rows), 0)
    at_key = lax.broadcasted_iota(jnp.int32, (ROWS, span_rows), 1)
    allowed = (at_key > at_row) & (at_key <= at_row + WINDOW) & (at_key + place * ROWS >= WINDOW)

    def attend(head, carry):
        cols = columns(head)
        queries = ql[:, cols]
        keys = jnp.concatenate([halo[0, :, cols], kl[:, cols]], 0)
        values = jnp.concatenate([halo[1, :, cols], vl[:, cols]], 0)
        for sub in range(HS // HEAD_DIM):
            part = slice(sub * HEAD_DIM, (sub + 1) * HEAD_DIM)
            scores = lax.dot_general(
                queries[:, part], keys[:, part], (((1,), (1,)), ((), ())), preferred_element_type=F32
            ) * (1.0 / math.sqrt(HEAD_DIM))
            masked = jnp.where(allowed, scores, -1e30)
            maximum = jnp.max(masked, axis=1, keepdims=True)
            weights = jnp.where(allowed, jnp.exp(masked - maximum), 0.0)
            totals = jnp.sum(weights, axis=1, keepdims=True)
            mixed = jnp.dot(weights.astype(BF16), values[:, part], preferred_element_type=F32)
            att[head, :, part] = mixed / totals
        return carry

    seven = far.at[pl.ds(0, NZ - 1)]
    remote(seven, seven, fsend, frecv, other).wait_recv()
    agb[c, spot] = jnp.sum(far[...].astype(F32), axis=0).astype(BF16)
    far_sends(agb, atsend, atrecv)
    near_sends(agb, atsend, atrecv, assend, asrecv)
    remote(halo, halo, hsend, hrecv, other).wait_recv()
    cross_sends(agb, assend, asrecv, afsend, afrecv, attend)
    crossed(agb, afsend, afrecv)

    def squares(i, total):
        for half in range(2):
            part = agb[half, pl.ds(i * NX, NX)].astype(F32).reshape(64, 3 * HS // 2)
            total = total + jnp.sum(part * part, axis=0, keepdims=True)
        return total

    square_sum = jnp.sum(lax.fori_loop(0, NZ, squares, jnp.zeros((1, 3 * HS // 2), F32)), axis=1, keepdims=True)
    step = STEP_SIZE * lax.rsqrt(square_sum * (1.0 / (3 * HS * HS)) + NORM_EPS)

    def renorm(i, carry):
        rows = pl.ds(pl.multiple_of(i * 64, 64), 64)
        low = agb[0, pl.ds(i * NX, NX)].astype(F32).reshape(64, 3 * HS // 2)
        high = agb[1, pl.ds(i * NX, NX)].astype(F32).reshape(64, 3 * HS // 2)
        for which in range(3):
            part = slice(which * HS // 2, (which + 1) * HS // 2)
            grads = jnp.concatenate([low[:, part], high[:, part]], 1)
            previous = wfull[rows, which * HS : (which + 1) * HS].astype(F32)
            stepped = previous - step * grads
            factor = jnp.sqrt(jnp.mean(previous * previous, axis=-1, keepdims=True)) * lax.rsqrt(
                jnp.mean(stepped * stepped, axis=-1, keepdims=True) + NORM_EPS
            )
            wnew[rows, which * HS : (which + 1) * HS] = (stepped * factor).astype(BF16)
        return carry

    lax.fori_loop(0, NZ, renorm, 0)

    for pair in range(4):
        queries = qb[2 * pair : 2 * pair + 2].reshape(2 * ROWS, HS)
        gate = jnp.dot(queries, wnew[:, :HS], preferred_element_type=F32)
        up = jnp.dot(queries, wnew[:, HS : 2 * HS], preferred_element_type=F32)
        hidden = (gate * jax.nn.sigmoid(gate) * up).astype(BF16)
        result = jnp.dot(hidden, wnew[:, 2 * HS :], preferred_element_type=F32)
        fo[2 * pair : 2 * pair + 2] = result.astype(BF16).reshape(2, ROWS, HS)
        for way in (2 * pair, 2 * pair + 1):
            if way < OWN:
                remote(fo.at[way], ret.at[way], osend, orecv.at[way], there(way, -1)).start()
    ret[OWN] = fo[OWN]
    for way in (OWN, *range(OWN)):
        if way < OWN:
            remote(ret.at[way], ret.at[way], osend, orecv.at[way], other).wait_recv()
        head = head_of(way)
        out_ref[:, columns(head)] = (att[head] + ret[way].astype(F32)).astype(BF16)

    for buffer, sem in ((kb, ksend), (vb, vsend), (qb, qsend), (ret, osend)):
        sent = buffer.at[pl.ds(0, OWN)]
        remote(sent, sent, sem, orecv.at[0], other).wait_send()
    remote(halo, halo, hsend, hrecv, other).wait_send()
    exchange.wait_send()
    for buffer, sem in ((near, nsend), (wrecv.at[0], wssend), (agb.at[0], assend)):
        sent = buffer.at[pl.ds(0, NZ * (NX - 1))]
        remote(sent, sent, sem, orecv.at[0], other).wait_send()
    for sem in (fsend, wtsend, atsend):
        remote(seven, seven, sem, orecv.at[0], other).wait_send()

    @pl.when(jnp.logical_not(is_self))
    def _():
        remote(wpack, wpack, wcsend, orecv.at[0], other).wait_send()

    for buffer, sem in ((wrecv.at[0], wfsend), (agb.at[0], afsend)):
        remote(buffer, buffer, sem, orecv.at[0], other).wait_send()


def shards(queries, key_rows, value_rows, step_rates, w_gate, w_up, w_down):
    hbm = pl.BlockSpec(memory_space=pl.ANY)
    vmem = pl.BlockSpec(memory_space=pltpu.VMEM)
    wide = 3 * HS // 2
    blocks = pltpu.VMEM((8, ROWS, HS), BF16)
    dma = pltpu.SemaphoreType.DMA
    return pl.pallas_call(
        fast_kernel,
        out_shape=jax.ShapeDtypeStruct((ROWS, D), BF16),
        in_specs=[hbm, hbm, hbm, vmem, vmem, vmem, vmem],
        out_specs=vmem,
        scratch_shapes=[
            pltpu.VMEM((ROWS, D), BF16),
            pltpu.VMEM((ROWS, D), BF16),
            pltpu.VMEM((ROWS, D), BF16),
            blocks,
            pltpu.VMEM((2, WINDOW, D), BF16),
            blocks,
            blocks,
            blocks,
            pltpu.VMEM((16, wide), BF16),
            pltpu.VMEM((2, NZ * NX, 16, wide), BF16),
            pltpu.VMEM((HS, 3 * HS), BF16),
            pltpu.VMEM((2, 8, ROWS, HS), BF16),
            blocks,
            pltpu.VMEM((HS, wide), F32),
            pltpu.VMEM((HS, wide), BF16),
            pltpu.VMEM((HS, wide), BF16),
            pltpu.VMEM((NZ * NX, 16, wide), BF16),
            pltpu.VMEM((NZ * NX, 16, wide), BF16),
            pltpu.VMEM((NZ, 16, wide), BF16),
            pltpu.VMEM((NZ, 16, wide), BF16),
            pltpu.VMEM((2, NZ * NX, 16, wide), BF16),
            pltpu.VMEM((HS, 3 * HS), BF16),
            blocks,
            blocks,
            pltpu.VMEM((8, ROWS, HS), F32),
            dma((3,)),
            dma, dma, dma, dma((NZ,)), dma, dma((NZ,)), dma, dma,
            dma, dma((OWN,)), dma, dma((OWN,)), dma, dma((OWN,)),
            dma, dma,
            dma, dma,
            dma, dma((NZ,)), dma, dma,
            dma, dma((NZ,)), dma, dma((NZ,)), dma, dma,
            dma, dma((OWN,)),
        ],
        compiler_params=pltpu.CompilerParams(collective_id=0, has_side_effects=True, vmem_limit_bytes=56 * 1024 * 1024),
    )(queries, key_rows, value_rows, jnp.transpose(step_rates), *(w.reshape(8, HS) for w in (w_gate, w_up, w_down)))


def solution(mesh):
    torus = Mesh(mesh.devices.reshape(NZ, 2, NX, 4, 2), AXES)
    seq = ("z", "yl", "x")
    head = ("yh", "c")
    return jax.shard_map(
        shards,
        mesh=torus,
        in_specs=(
            P((*seq, *head), None),
            P((*seq, *head), None),
            P((*seq, *head), None),
            P((*seq, *head), None),
            P(seq, head, None),
            P(seq, head, None),
            P(seq, head, None),
        ),
        out_specs=P((*seq, *head), None),
        check_vma=False,
    )
```

```python
import math

import jax
import jax.numpy as jnp
from jax import lax
from jax.experimental import pallas as pl
from jax.experimental.pallas import tpu as pltpu
from jax.sharding import Mesh
from jax.sharding import PartitionSpec as P

HEAD_DIM = 128
HEADS = 8
HS = 512
WINDOW = 64
STEP_SIZE = 0.05
NORM_EPS = 1e-06
ROWS = 128
D = HEADS * HS
NX, NY, NZ = 4, 8, 8
AXES = ("z", "yl", "x", "yh", "c")
MESH = pl.DeviceIdType.MESH
F32, BF16 = jnp.float32, jnp.bfloat16
WAYS = ((1, 0, 1, 0), (7, 0, -1, 0), (3, 0, 0, 1), (5, 0, 0, -1), (2, 1, 0, 0), (6, -1, 0, 0), (4, 0, 1, 1))
OWN = len(WAYS)


def fast_kernel(
    q_hbm, k_hbm, v_hbm, rate_ref, wg_ref, wu_ref, wd_ref, out_ref,
    ql, kl, vl, tl, edge_q, edge_o, edge_in, stat_o, stat_in, stat_own, kb, vb, qb, wpack, wrecv, wfull, gu, hid, gown, gsend, gex, gb, near, part_sum, far, agb, wnew, fo, ret, att,
    lsem, wcsend, wcrecv, wtsend, wtrecv, wssend, wsrecv, wfsend, wfrecv, ksend, krecv, vsend, vrecv, qsend, qrecv,
    hqsend, hqrecv, hosend, horecv, hssend, hsrecv, exsend, exrecv, nsend, nrecv, fsend, frecv, atsend, atrecv, assend, asrecv, afsend, afrecv, osend, orecv,
):
    z, yl, x, yh, c = (lax.axis_index(a) for a in AXES)
    y = 2 * yh + yl
    colour = lax.rem(2 * x + y + 3 * z, 8)
    sign = 1 - 2 * c
    other = (z, yl, x, yh, 1 - c)
    skew = 2 * (1 - c)
    line = lax.rem(z - skew * x + 64, NZ)
    spot = line * NX + x
    place = (((z * 2 + yl) * NX + x) * 4 + yh) * 2 + c

    def device(px, py, pz, core):
        py = lax.rem(py + 64, NY)
        return (lax.rem(pz + 64, NZ), lax.rem(py, 2), lax.rem(px + 64, NX), py // 2, core)

    def there(way, back=1):
        _, dx, dy, dz = WAYS[way]
        turn = sign if way == OWN - 1 else 1
        return device(x + back * dx, y + back * turn * dy, z + back * turn * dz, c)

    def head_of(way):
        return colour if way == OWN else lax.rem(colour + WAYS[way][0], 8)

    def remote(src, dst, send, recv, dev):
        return pltpu.make_async_remote_copy(
            src_ref=src, dst_ref=dst, send_sem=send, recv_sem=recv, device_id=dev, device_id_type=MESH
        )

    def columns(head):
        return pl.ds(pl.multiple_of(head * HS, HS), HS)

    def near_mate(step):
        dz = skew * step
        return device(x + step, y - 2 * step - 3 * dz, z + dz, c)

    def far_mate(step):
        return device(x, y - 3 * step, z + step, c)

    def block_at(index):
        index = lax.rem(index + 512, 512)
        return (index // 64, lax.rem(index // 32, 2), lax.rem(index // 8, 4), lax.rem(index // 2, 4), lax.rem(index, 2))

    my_head = 2 * yh + c
    is_self = (my_head == colour) & (yl == c)
    weight_dest = device(x, my_head - 2 * x - 3 * z, z, yl)
    weight_source = (z, c, x, colour // 2, lax.rem(colour, 2))

    barrier = pltpu.get_barrier_semaphore()
    partners = [there(way) for way in range(OWN)] + [there(OWN - 1, -1), other, block_at(place + 1), block_at(place - 1)]
    partners += [near_mate(step) for step in range(1, NX)] + [far_mate(step) for step in range(1, NZ)]

    def greet(dev):
        pl.semaphore_signal(barrier, inc=1, device_id=dev, device_id_type=MESH)

    for dev in partners:
        greet(dev)

    @pl.when(jnp.logical_not(is_self))
    def _():
        greet(weight_dest)
        greet(weight_source)

    loads = [pltpu.make_async_copy(v_hbm, vl, lsem.at[0]), pltpu.make_async_copy(k_hbm, kl, lsem.at[1]),
             pltpu.make_async_copy(q_hbm, ql, lsem.at[2])]
    for load in loads:
        load.start()
    gate_rows, up_rows, down_rows = (ref[...].astype(F32) for ref in (wg_ref, wu_ref, wd_ref))
    wpack[...] = jnp.concatenate(
        [jnp.concatenate([gate_rows, up_rows[:, : HS // 2]], 1), jnp.concatenate([up_rows[:, HS // 2 :], down_rows], 1)], 0
    ).astype(BF16)

    @pl.when(is_self)
    def _():
        pl.semaphore_wait(barrier, len(partners))

    @pl.when(jnp.logical_not(is_self))
    def _():
        pl.semaphore_wait(barrier, len(partners) + 2)

    dest_spot = lax.rem(z - 2 * (1 - yl) * x + 64, NZ) * NX + x

    @pl.when(is_self)
    def _():
        wrecv[yl, dest_spot] = wpack[...]

    @pl.when(jnp.logical_not(is_self))
    def _():
        remote(wpack, wrecv.at[yl, dest_spot], wcsend, wcrecv, weight_dest).start()

    for way in range(OWN):
        remote(k_hbm.at[:, columns(head_of(way))], kb.at[way], ksend, krecv.at[way], there(way)).start()

    def far_sends(buffer, send, recv):
        def go(step, carry):
            block = buffer.at[c, spot]
            remote(block, block, send, recv.at[step], far_mate(step)).start()
            return carry

        lax.fori_loop(1, NZ, go, 0)

    def near_sends(buffer, send, recv, nsend_, nrecv_):
        def go(step, carry):
            block = buffer.at[c, lax.rem(line - step + NZ, NZ) * NX + x]

            @pl.when(step > 0)
            def _():
                remote(block, block, send, recv.at[step], other).wait_recv()

            for move in range(1, NX):
                remote(block, block, nsend_, nrecv_.at[step], near_mate(move)).start()
            return carry

        lax.fori_loop(0, NZ, go, 0)

    def cross_sends(buffer, nsend_, nrecv_, csend, crecv, beside=None):
        def go(step, carry):
            if beside is not None:
                beside(step, 0)
            three = buffer.at[c, pl.ds(0, NX - 1)]
            remote(three, three, nsend_, nrecv_.at[step], other).wait_recv()
            four = buffer.at[c, pl.ds(lax.rem(line - step + NZ, NZ) * NX, NX)]
            remote(four, four, csend, crecv, other).start()
            return carry

        lax.fori_loop(0, NZ, go, 0)

    def crossed(buffer, csend, crecv):
        remote(buffer.at[1 - c], buffer.at[1 - c], csend, crecv, other).wait_recv()

    @pl.when(jnp.logical_not(is_self))
    def _():
        remote(wpack, wpack, wcsend, wcrecv, other).wait_recv()

    far_sends(wrecv, wtsend, wtrecv)
    rates = jnp.transpose(rate_ref[...].astype(F32))
    loads[0].wait()
    for head in range(HEADS):
        rate = rates[:, head : head + 1]
        tl[head] = (-rate * vl[:, head * HS : (head + 1) * HS].astype(F32)).astype(BF16)
    for way in range(OWN):
        remote(tl.at[head_of(way)], vb.at[way], vsend, vrecv.at[way], there(way)).start()
    vb[OWN] = tl[colour]
    loads[1].wait()
    kb[OWN] = kl[:, columns(colour)]

    near_sends(wrecv, wtsend, wtrecv, wssend, wsrecv)

    def unpack(half):
        def rows_of(pz, carry):
            for px in range(0, NX, 2):
                one, two = (
                    wrecv[half, lax.rem(pz - 2 * (1 - half) * at + 64, NZ) * NX + at].astype(F32) for at in (px, px + 1)
                )
                rows = pl.ds(pl.multiple_of(((pz * 2 + half) * NX + px) * 8, 16), 16)
                wfull[rows, : 3 * HS // 2] = jnp.concatenate([one[:8], two[:8]], 0).astype(BF16)
                wfull[rows, 3 * HS // 2 :] = jnp.concatenate([one[8:], two[8:]], 0).astype(BF16)
            return carry

        lax.fori_loop(0, NZ, rows_of, 0)

    def normed(block):
        wide = block.astype(F32)
        return (wide * lax.rsqrt(jnp.mean(wide * wide, axis=-1, keepdims=True) + NORM_EPS)).astype(BF16)

    for way in range(OWN + 1):
        if way < OWN:
            remote(kb.at[way], kb.at[way], ksend, krecv.at[way], other).wait_recv()
        kb[way] = normed(kb[way])

    cross_sends(wrecv, wssend, wsrecv, wfsend, wfrecv)
    unpack(c)
    crossed(wrecv, wfsend, wfrecv)
    unpack(1 - c)

    for way in range(OWN):
        remote(vb.at[way], vb.at[way], vsend, vrecv.at[way], other).wait_recv()

    for way in range(OWN):
        remote(q_hbm.at[:, columns(head_of(way))], qb.at[way], qsend, qrecv.at[way], there(way)).start()
    edge = q_hbm.at[pl.ds(0, WINDOW)]
    remote(edge, edge_q, hqsend, hqrecv, block_at(place - 1)).start()
    loads[2].wait()
    qb[OWN] = normed(ql[:, columns(colour)])

    def tokens(i, carry):
        keys = kb[pl.ds(2 * i, 2)].reshape(2 * ROWS, HS)
        target = vb[pl.ds(2 * i, 2)].reshape(2 * ROWS, HS)
        gate_pre = jnp.dot(keys, wfull[:, :HS], preferred_element_type=F32)
        up_pre = jnp.dot(keys, wfull[:, HS : 2 * HS], preferred_element_type=F32)
        hidden_grad = lax.dot_general(
            target, wfull[:, 2 * HS :], (((1,), (1,)), ((), ())), preferred_element_type=F32
        )
        sigma = jax.nn.sigmoid(gate_pre)
        silu = gate_pre * sigma
        hid[pl.ds(2 * i, 2)] = (silu * up_pre).astype(BF16).reshape(2, ROWS, HS)
        gate_grad = (hidden_grad * up_pre * sigma * (1.0 + gate_pre * (1.0 - sigma))).astype(BF16)
        up_grad = (hidden_grad * silu).astype(BF16)
        for half in range(2):
            part = slice(half * HS // 2, (half + 1) * HS // 2)
            gu[half, pl.ds(2 * i, 2), :, : HS // 2] = gate_grad[:, part].reshape(2, ROWS, HS // 2)
            gu[half, pl.ds(2 * i, 2), :, HS // 2 :] = up_grad[:, part].reshape(2, ROWS, HS // 2)
        return carry

    lax.fori_loop(0, 4, tokens, 0)

    def half_sums(half, store):
        def rows(i, carry):
            span = pl.ds(pl.multiple_of(i * 256, 256), 256)
            keys = kb[:, :, span].reshape(8 * ROWS, 256)
            grads = gu[half].reshape(8 * ROWS, HS)
            hidden = hid[:, :, span].reshape(8 * ROWS, 256)
            target = vb[:, :, pl.ds(pl.multiple_of(half * 256, 256), 256)].reshape(8 * ROWS, 256)
            over_tokens = (((0,), (0,)), ((), ()))
            store[span, :HS] = lax.dot_general(keys, grads, over_tokens, preferred_element_type=F32).astype(store.dtype)
            store[span, HS:] = lax.dot_general(hidden, target, over_tokens, preferred_element_type=F32).astype(store.dtype)
            return carry

        lax.fori_loop(0, 2, rows, 0)

    half_sums(1 - c, gsend)
    exchange = remote(gsend, gex, exsend, exrecv, other)
    exchange.start()
    half_sums(c, gown)
    exchange.wait_recv()

    scale = 1.0 / math.sqrt(HEAD_DIM)
    by_column = (((1,), (1,)), ((), ()))
    edge_row = lax.broadcasted_iota(jnp.int32, (WINDOW, WINDOW), 0)
    edge_key = lax.broadcasted_iota(jnp.int32, (WINDOW, WINDOW), 1)
    in_window = edge_key > edge_row
    stat_lane = lax.broadcasted_iota(jnp.int32, (WINDOW, HEAD_DIM), 1)
    next_block = block_at(place + 1)
    stat_o[...] = jnp.zeros_like(stat_o)

    def attend_edge(head, carry):
        cols = columns(head)
        queries = edge_q[:, cols]
        keys, values = (ref[pl.ds(ROWS - WINDOW, WINDOW), cols] for ref in (kl, vl))
        stats = stat_o[...]
        for sub in range(HS // HEAD_DIM):
            part = slice(sub * HEAD_DIM, (sub + 1) * HEAD_DIM)
            scores = lax.dot_general(queries[:, part], keys[:, part], by_column, preferred_element_type=F32) * scale
            masked = jnp.where(in_window, scores, -1e30)
            maximum = jnp.max(masked, axis=1, keepdims=True)
            weights = jnp.where(in_window, jnp.exp(masked - maximum), 0.0)
            totals = jnp.sum(weights, axis=1, keepdims=True)
            edge_o[head, :, part] = jnp.dot(weights.astype(BF16), values[:, part], preferred_element_type=F32).astype(BF16)
            lane = head * (HS // HEAD_DIM) + sub
            stats = jnp.where(stat_lane == lane, maximum, jnp.where(stat_lane == lane + 32, totals, stats))
        stat_o[...] = stats
        return carry

    at_row = lax.broadcasted_iota(jnp.int32, (ROWS, ROWS), 0)
    at_key = lax.broadcasted_iota(jnp.int32, (ROWS, ROWS), 1)
    allowed = (at_key > at_row - WINDOW) & (at_key <= at_row)

    def attend(head):
        cols = columns(head)
        queries, keys, values = ql[:, cols], kl[:, cols], vl[:, cols]
        stats = jnp.zeros((WINDOW, HEAD_DIM), F32)
        for sub in range(HS // HEAD_DIM):
            part = slice(sub * HEAD_DIM, (sub + 1) * HEAD_DIM)
            scores = lax.dot_general(queries[:, part], keys[:, part], by_column, preferred_element_type=F32) * scale
            masked = jnp.where(allowed, scores, -1e30)
            maximum = jnp.max(masked, axis=1, keepdims=True)
            weights = jnp.where(allowed, jnp.exp(masked - maximum), 0.0)
            totals = jnp.sum(weights, axis=1, keepdims=True)
            mixed = jnp.dot(weights.astype(BF16), values[:, part], preferred_element_type=F32)
            stats = jnp.where(
                stat_lane == sub, maximum[:WINDOW], jnp.where(stat_lane == sub + 4, totals[:WINDOW], stats)
            )
            att[head, :WINDOW, part] = mixed[:WINDOW]
            att[head, WINDOW:, part] = mixed[WINDOW:] / totals[WINDOW:]
        stat_own[head] = stats

    def merge(head, carry):
        stats, own = stat_in[...], stat_own[head]
        for sub in range(HS // HEAD_DIM):
            part = slice(sub * HEAD_DIM, (sub + 1) * HEAD_DIM)
            lane = head * (HS // HEAD_DIM) + sub
            edge_max, edge_total = (
                jnp.sum(jnp.where(stat_lane == at, stats, 0.0), axis=1, keepdims=True) for at in (lane, lane + 32)
            )
            edge_max = jnp.where(place == 0, -1e30, edge_max)
            maximum, totals = own[:, sub : sub + 1], own[:, sub + 4 : sub + 5]
            both_max = jnp.maximum(maximum, edge_max)
            here, before = jnp.exp(maximum - both_max), jnp.exp(edge_max - both_max)
            first = att[head, :WINDOW, part] * here + edge_in[head, :, part].astype(F32) * before
            att[head, :WINDOW, part] = first / (totals * here + edge_total * before)
        return carry

    def near_sums(i, carry):
        step = lax.rem(i + 1, NZ)
        to = lax.rem(line + step, NZ)
        rows = pl.ds(pl.multiple_of(to * 64, 64), 64)
        gb[pl.ds(to * NX, NX)] = (gown[rows, :] + gex[rows, :].astype(F32)).astype(BF16).reshape(NX, 16, 3 * HS // 2)
        for move in range(1, NX):
            block = gb.at[to * NX + lax.rem(x + move, NX)]
            remote(block, near.at[to * NX + x], nsend, nrecv.at[step], near_mate(move)).start()
        return carry

    lax.fori_loop(0, NZ, near_sums, 0)

    for way in range(OWN):
        remote(qb.at[way], qb.at[way], qsend, qrecv.at[way], other).wait_recv()
        qb[way] = normed(qb[way])

    def far_sums(i, carry):
        attend(i)
        step = lax.rem(i + 1, NZ)
        to = lax.rem(line + step, NZ)
        three = near.at[pl.ds(0, NX - 1)]
        remote(three, three, nsend, nrecv.at[step], other).wait_recv()
        near[to * NX + x] = gb[to * NX + x]
        part_sum[to] = jnp.sum(near[pl.ds(to * NX, NX)].astype(F32), axis=0).astype(BF16)

        @pl.when(step > 0)
        def _():
            remote(part_sum.at[to], far.at[line], fsend, frecv, far_mate(step)).start()

        return carry

    lax.fori_loop(0, NZ, far_sums, 0)
    far[line] = part_sum[line]

    seven = far.at[pl.ds(0, NZ - 1)]
    remote(seven, seven, fsend, frecv, other).wait_recv()
    agb[c, spot] = jnp.sum(far[...].astype(F32), axis=0).astype(BF16)
    far_sends(agb, atsend, atrecv)
    near_sends(agb, atsend, atrecv, assend, asrecv)
    remote(edge_q, edge_q, hqsend, hqrecv, other).wait_recv()
    cross_sends(agb, assend, asrecv, afsend, afrecv, attend_edge)
    remote(edge_o, edge_in, hosend, horecv, next_block).start()
    remote(stat_o, stat_in, hssend, hsrecv, next_block).start()
    crossed(agb, afsend, afrecv)

    def squares(i, total):
        for half in range(2):
            part = agb[half, pl.ds(i * NX, NX)].astype(F32).reshape(64, 3 * HS // 2)
            total = total + jnp.sum(part * part, axis=0, keepdims=True)
        return total

    square_sum = jnp.sum(lax.fori_loop(0, NZ, squares, jnp.zeros((1, 3 * HS // 2), F32)), axis=1, keepdims=True)
    step = STEP_SIZE * lax.rsqrt(square_sum * (1.0 / (3 * HS * HS)) + NORM_EPS)

    def renorm(i, carry):
        rows = pl.ds(pl.multiple_of(i * 64, 64), 64)
        low = agb[0, pl.ds(i * NX, NX)].astype(F32).reshape(64, 3 * HS // 2)
        high = agb[1, pl.ds(i * NX, NX)].astype(F32).reshape(64, 3 * HS // 2)
        for which in range(3):
            part = slice(which * HS // 2, (which + 1) * HS // 2)
            grads = jnp.concatenate([low[:, part], high[:, part]], 1)
            previous = wfull[rows, which * HS : (which + 1) * HS].astype(F32)
            stepped = previous - step * grads
            factor = jnp.sqrt(jnp.mean(previous * previous, axis=-1, keepdims=True)) * lax.rsqrt(
                jnp.mean(stepped * stepped, axis=-1, keepdims=True) + NORM_EPS
            )
            wnew[rows, which * HS : (which + 1) * HS] = (stepped * factor).astype(BF16)
        return carry

    lax.fori_loop(0, NZ, renorm, 0)

    for pair in range(4):
        queries = qb[2 * pair : 2 * pair + 2].reshape(2 * ROWS, HS)
        gate = jnp.dot(queries, wnew[:, :HS], preferred_element_type=F32)
        up = jnp.dot(queries, wnew[:, HS : 2 * HS], preferred_element_type=F32)
        hidden = (gate * jax.nn.sigmoid(gate) * up).astype(BF16)
        result = jnp.dot(hidden, wnew[:, 2 * HS :], preferred_element_type=F32)
        fo[2 * pair : 2 * pair + 2] = result.astype(BF16).reshape(2, ROWS, HS)
        for way in (2 * pair, 2 * pair + 1):
            if way < OWN:
                remote(fo.at[way], ret.at[way], osend, orecv.at[way], there(way, -1)).start()
    remote(edge_in, edge_in, hosend, horecv, other).wait_recv()
    remote(stat_in, stat_in, hssend, hsrecv, other).wait_recv()
    lax.fori_loop(0, HEADS, merge, 0)
    ret[OWN] = fo[OWN]
    for way in (OWN, *range(OWN)):
        if way < OWN:
            remote(ret.at[way], ret.at[way], osend, orecv.at[way], other).wait_recv()
        head = head_of(way)
        out_ref[:, columns(head)] = (att[head] + ret[way].astype(F32)).astype(BF16)

    for buffer, sem in ((kb, ksend), (vb, vsend), (qb, qsend), (ret, osend)):
        sent = buffer.at[pl.ds(0, OWN)]
        remote(sent, sent, sem, orecv.at[0], other).wait_send()
    for buffer, sem in ((edge_q, hqsend), (edge_in, hosend), (stat_in, hssend)):
        remote(buffer, buffer, sem, orecv.at[0], other).wait_send()
    exchange.wait_send()
    for buffer, sem in ((near, nsend), (wrecv.at[0], wssend), (agb.at[0], assend)):
        sent = buffer.at[pl.ds(0, NZ * (NX - 1))]
        remote(sent, sent, sem, orecv.at[0], other).wait_send()
    for sem in (fsend, wtsend, atsend):
        remote(seven, seven, sem, orecv.at[0], other).wait_send()

    @pl.when(jnp.logical_not(is_self))
    def _():
        remote(wpack, wpack, wcsend, orecv.at[0], other).wait_send()

    for buffer, sem in ((wrecv.at[0], wfsend), (agb.at[0], afsend)):
        remote(buffer, buffer, sem, orecv.at[0], other).wait_send()


def shards(queries, key_rows, value_rows, step_rates, w_gate, w_up, w_down):
    hbm = pl.BlockSpec(memory_space=pl.ANY)
    vmem = pl.BlockSpec(memory_space=pltpu.VMEM)
    wide = 3 * HS // 2
    blocks = pltpu.VMEM((8, ROWS, HS), BF16)
    dma = pltpu.SemaphoreType.DMA
    return pl.pallas_call(
        fast_kernel,
        out_shape=jax.ShapeDtypeStruct((ROWS, D), BF16),
        in_specs=[hbm, hbm, hbm, vmem, vmem, vmem, vmem],
        out_specs=vmem,
        scratch_shapes=[
            pltpu.VMEM((ROWS, D), BF16),
            pltpu.VMEM((ROWS, D), BF16),
            pltpu.VMEM((ROWS, D), BF16),
            blocks,
            pltpu.VMEM((WINDOW, D), BF16),
            pltpu.VMEM((8, WINDOW, HS), BF16),
            pltpu.VMEM((8, WINDOW, HS), BF16),
            pltpu.VMEM((WINDOW, HEAD_DIM), F32),
            pltpu.VMEM((WINDOW, HEAD_DIM), F32),
            pltpu.VMEM((8, WINDOW, HEAD_DIM), F32),
            blocks,
            blocks,
            blocks,
            pltpu.VMEM((16, wide), BF16),
            pltpu.VMEM((2, NZ * NX, 16, wide), BF16),
            pltpu.VMEM((HS, 3 * HS), BF16),
            pltpu.VMEM((2, 8, ROWS, HS), BF16),
            blocks,
            pltpu.VMEM((HS, wide), F32),
            pltpu.VMEM((HS, wide), BF16),
            pltpu.VMEM((HS, wide), BF16),
            pltpu.VMEM((NZ * NX, 16, wide), BF16),
            pltpu.VMEM((NZ * NX, 16, wide), BF16),
            pltpu.VMEM((NZ, 16, wide), BF16),
            pltpu.VMEM((NZ, 16, wide), BF16),
            pltpu.VMEM((2, NZ * NX, 16, wide), BF16),
            pltpu.VMEM((HS, 3 * HS), BF16),
            blocks,
            blocks,
            pltpu.VMEM((8, ROWS, HS), F32),
            dma((3,)),
            dma, dma, dma, dma((NZ,)), dma, dma((NZ,)), dma, dma,
            dma, dma((OWN,)), dma, dma((OWN,)), dma, dma((OWN,)),
            dma, dma, dma, dma, dma, dma,
            dma, dma,
            dma, dma((NZ,)), dma, dma,
            dma, dma((NZ,)), dma, dma((NZ,)), dma, dma,
            dma, dma((OWN,)),
        ],
        compiler_params=pltpu.CompilerParams(collective_id=0, has_side_effects=True, vmem_limit_bytes=56 * 1024 * 1024),
    )(queries, key_rows, value_rows, jnp.transpose(step_rates), *(w.reshape(8, HS) for w in (w_gate, w_up, w_down)))


def solution(mesh):
    torus = Mesh(mesh.devices.reshape(NZ, 2, NX, 4, 2), AXES)
    seq = ("z", "yl", "x")
    head = ("yh", "c")
    return jax.shard_map(
        shards,
        mesh=torus,
        in_specs=(
            P((*seq, *head), None),
            P((*seq, *head), None),
            P((*seq, *head), None),
            P((*seq, *head), None),
            P(seq, head, None),
            P(seq, head, None),
            P(seq, head, None),
        ),
        out_specs=P((*seq, *head), None),
        check_vma=False,
    )
```

```python
import math

import jax
import jax.numpy as jnp
from jax import lax
from jax.experimental import pallas as pl
from jax.experimental.pallas import tpu as pltpu
from jax.sharding import Mesh
from jax.sharding import PartitionSpec as P

HEAD_DIM = 128
HEADS = 8
HS = 512
WINDOW = 64
STEP_SIZE = 0.05
NORM_EPS = 1e-06
ROWS = 128
D = HEADS * HS
NX, NY, NZ = 4, 8, 8
AXES = ("z", "yl", "x", "yh", "c")
MESH = pl.DeviceIdType.MESH
F32, BF16 = jnp.float32, jnp.bfloat16
WAYS = ((1, 0, 1, 0), (7, 0, -1, 0), (3, 0, 0, 1), (5, 0, 0, -1), (2, 1, 0, 0), (6, -1, 0, 0), (4, 0, 1, 1))
OWN = len(WAYS)


def fast_kernel(
    q_hbm, k_hbm, v_hbm, rate_ref, wg_ref, wu_ref, wd_ref, out_ref,
    ql, kl, vl, tl, edge_q, edge_o, edge_in, stat_o, stat_in, stat_own, kb, vb, qb, wpack, wrecv, wfull, gu, hid, gown, gsend, gex, gb, near, part_sum, far, agb, wnew, fo, ret, att,
    lsem, wcsend, wcrecv, wtsend, wtrecv, wssend, wsrecv, wfsend, wfrecv, ksend, krecv, vsend, vrecv, qsend, qrecv,
    hqsend, hqrecv, hosend, horecv, hssend, hsrecv, exsend, exrecv, nsend, nrecv, fsend, frecv, atsend, atrecv, assend, asrecv, afsend, afrecv, osend, orecv,
):
    z, yl, x, yh, c = (lax.axis_index(a) for a in AXES)
    y = 2 * yh + yl
    colour = lax.rem(2 * x + y + 3 * z, 8)
    sign = 1 - 2 * c
    other = (z, yl, x, yh, 1 - c)
    skew = 2 * (1 - c)
    line = lax.rem(z - skew * x + 64, NZ)
    spot = line * NX + x
    place = (((z * 2 + yl) * NX + x) * 4 + yh) * 2 + c

    def device(px, py, pz, core):
        py = lax.rem(py + 64, NY)
        return (lax.rem(pz + 64, NZ), lax.rem(py, 2), lax.rem(px + 64, NX), py // 2, core)

    def there(way, back=1):
        _, dx, dy, dz = WAYS[way]
        turn = sign if way == OWN - 1 else 1
        return device(x + back * dx, y + back * turn * dy, z + back * turn * dz, c)

    def head_of(way):
        return colour if way == OWN else lax.rem(colour + WAYS[way][0], 8)

    def remote(src, dst, send, recv, dev):
        return pltpu.make_async_remote_copy(
            src_ref=src, dst_ref=dst, send_sem=send, recv_sem=recv, device_id=dev, device_id_type=MESH
        )

    def columns(head):
        return pl.ds(pl.multiple_of(head * HS, HS), HS)

    def near_mate(step):
        dz = skew * step
        return device(x + step, y - 2 * step - 3 * dz, z + dz, c)

    def far_mate(step):
        return device(x, y - 3 * step, z + step, c)

    def block_at(index):
        index = lax.rem(index + 512, 512)
        return (index // 64, lax.rem(index // 32, 2), lax.rem(index // 8, 4), lax.rem(index // 2, 4), lax.rem(index, 2))

    my_head = 2 * yh + c
    is_self = (my_head == colour) & (yl == c)
    weight_dest = device(x, my_head - 2 * x - 3 * z, z, yl)
    weight_source = (z, c, x, colour // 2, lax.rem(colour, 2))

    barrier = pltpu.get_barrier_semaphore()
    partners = [there(way) for way in range(OWN)] + [there(OWN - 1, -1), other, block_at(place + 1), block_at(place - 1)]
    partners += [near_mate(step) for step in range(1, NX)] + [far_mate(step) for step in range(1, NZ)]

    def greet(dev):
        pl.semaphore_signal(barrier, inc=1, device_id=dev, device_id_type=MESH)

    for dev in partners:
        greet(dev)

    @pl.when(jnp.logical_not(is_self))
    def _():
        greet(weight_dest)
        greet(weight_source)

    loads = [pltpu.make_async_copy(v_hbm, vl, lsem.at[0]), pltpu.make_async_copy(k_hbm, kl, lsem.at[1]),
             pltpu.make_async_copy(q_hbm, ql, lsem.at[2])]
    for load in loads:
        load.start()
    gate_rows, up_rows, down_rows = (ref[...].astype(F32) for ref in (wg_ref, wu_ref, wd_ref))
    wpack[...] = jnp.concatenate(
        [jnp.concatenate([gate_rows, up_rows[:, : HS // 2]], 1), jnp.concatenate([up_rows[:, HS // 2 :], down_rows], 1)], 0
    ).astype(BF16)

    @pl.when(is_self)
    def _():
        pl.semaphore_wait(barrier, len(partners))

    @pl.when(jnp.logical_not(is_self))
    def _():
        pl.semaphore_wait(barrier, len(partners) + 2)

    dest_spot = lax.rem(z - 2 * (1 - yl) * x + 64, NZ) * NX + x

    @pl.when(is_self)
    def _():
        wrecv[yl, dest_spot] = wpack[...]

    @pl.when(jnp.logical_not(is_self))
    def _():
        remote(wpack, wrecv.at[yl, dest_spot], wcsend, wcrecv, weight_dest).start()

    for way in range(OWN):
        remote(k_hbm.at[:, columns(head_of(way))], kb.at[way], ksend, krecv.at[way], there(way)).start()

    def far_sends(buffer, send, recv):
        def go(step, carry):
            block = buffer.at[c, spot]
            remote(block, block, send, recv.at[step], far_mate(step)).start()
            return carry

        lax.fori_loop(1, NZ, go, 0)

    def near_sends(buffer, send, recv, nsend_, nrecv_):
        def go(step, carry):
            block = buffer.at[c, lax.rem(line - step + NZ, NZ) * NX + x]

            @pl.when(step > 0)
            def _():
                remote(block, block, send, recv.at[step], other).wait_recv()

            for move in range(1, NX):
                remote(block, block, nsend_, nrecv_.at[step], near_mate(move)).start()
            return carry

        lax.fori_loop(0, NZ, go, 0)

    def cross_sends(buffer, nsend_, nrecv_, csend, crecv, beside=None):
        def go(step, carry):
            if beside is not None:
                beside(step, 0)
            three = buffer.at[c, pl.ds(0, NX - 1)]
            remote(three, three, nsend_, nrecv_.at[step], other).wait_recv()
            four = buffer.at[c, pl.ds(lax.rem(line - step + NZ, NZ) * NX, NX)]
            remote(four, four, csend, crecv, other).start()
            return carry

        lax.fori_loop(0, NZ, go, 0)

    def crossed(buffer, csend, crecv):
        remote(buffer.at[1 - c], buffer.at[1 - c], csend, crecv, other).wait_recv()

    @pl.when(jnp.logical_not(is_self))
    def _():
        remote(wpack, wpack, wcsend, wcrecv, other).wait_recv()

    far_sends(wrecv, wtsend, wtrecv)
    rates = jnp.transpose(rate_ref[...].astype(F32))
    loads[0].wait()
    for head in range(HEADS):
        rate = rates[:, head : head + 1]
        tl[head] = (-rate * vl[:, head * HS : (head + 1) * HS].astype(F32)).astype(BF16)
    for way in range(OWN):
        remote(tl.at[head_of(way)], vb.at[way], vsend, vrecv.at[way], there(way)).start()
    vb[OWN] = tl[colour]
    loads[1].wait()
    kb[OWN] = kl[:, columns(colour)]

    near_sends(wrecv, wtsend, wtrecv, wssend, wsrecv)

    def unpack(half):
        def rows_of(pz, carry):
            for px in range(0, NX, 2):
                one, two = (
                    wrecv[half, lax.rem(pz - 2 * (1 - half) * at + 64, NZ) * NX + at].astype(F32) for at in (px, px + 1)
                )
                rows = pl.ds(pl.multiple_of(((pz * 2 + half) * NX + px) * 8, 16), 16)
                wfull[rows, : 3 * HS // 2] = jnp.concatenate([one[:8], two[:8]], 0).astype(BF16)
                wfull[rows, 3 * HS // 2 :] = jnp.concatenate([one[8:], two[8:]], 0).astype(BF16)
            return carry

        lax.fori_loop(0, NZ, rows_of, 0)

    def normed(block):
        wide = block.astype(F32)
        return (wide * lax.rsqrt(jnp.mean(wide * wide, axis=-1, keepdims=True) + NORM_EPS)).astype(BF16)

    for way in range(OWN + 1):
        if way < OWN:
            remote(kb.at[way], kb.at[way], ksend, krecv.at[way], other).wait_recv()
        kb[way] = normed(kb[way])

    cross_sends(wrecv, wssend, wsrecv, wfsend, wfrecv)
    unpack(c)
    crossed(wrecv, wfsend, wfrecv)
    unpack(1 - c)

    for way in range(OWN):
        remote(vb.at[way], vb.at[way], vsend, vrecv.at[way], other).wait_recv()

    edge = q_hbm.at[pl.ds(0, WINDOW)]
    remote(edge, edge_q, hqsend, hqrecv, block_at(place - 1)).start()
    loads[2].wait()
    qb[OWN] = normed(ql[:, columns(colour)])

    def tokens(i, carry):
        keys = kb[pl.ds(2 * i, 2)].reshape(2 * ROWS, HS)
        target = vb[pl.ds(2 * i, 2)].reshape(2 * ROWS, HS)
        gate_pre = jnp.dot(keys, wfull[:, :HS], preferred_element_type=F32)
        up_pre = jnp.dot(keys, wfull[:, HS : 2 * HS], preferred_element_type=F32)
        hidden_grad = lax.dot_general(
            target, wfull[:, 2 * HS :], (((1,), (1,)), ((), ())), preferred_element_type=F32
        )
        sigma = jax.nn.sigmoid(gate_pre)
        silu = gate_pre * sigma
        hid[pl.ds(2 * i, 2)] = (silu * up_pre).astype(BF16).reshape(2, ROWS, HS)
        gate_grad = (hidden_grad * up_pre * sigma * (1.0 + gate_pre * (1.0 - sigma))).astype(BF16)
        up_grad = (hidden_grad * silu).astype(BF16)
        for half in range(2):
            part = slice(half * HS // 2, (half + 1) * HS // 2)
            gu[half, pl.ds(2 * i, 2), :, : HS // 2] = gate_grad[:, part].reshape(2, ROWS, HS // 2)
            gu[half, pl.ds(2 * i, 2), :, HS // 2 :] = up_grad[:, part].reshape(2, ROWS, HS // 2)
        return carry

    lax.fori_loop(0, 4, tokens, 0)

    def half_sums(half, store):
        def rows(i, carry):
            span = pl.ds(pl.multiple_of(i * 256, 256), 256)
            keys = kb[:, :, span].reshape(8 * ROWS, 256)
            grads = gu[half].reshape(8 * ROWS, HS)
            hidden = hid[:, :, span].reshape(8 * ROWS, 256)
            target = vb[:, :, pl.ds(pl.multiple_of(half * 256, 256), 256)].reshape(8 * ROWS, 256)
            over_tokens = (((0,), (0,)), ((), ()))
            store[span, :HS] = lax.dot_general(keys, grads, over_tokens, preferred_element_type=F32).astype(store.dtype)
            store[span, HS:] = lax.dot_general(hidden, target, over_tokens, preferred_element_type=F32).astype(store.dtype)
            return carry

        lax.fori_loop(0, 2, rows, 0)

    half_sums(1 - c, gsend)
    exchange = remote(gsend, gex, exsend, exrecv, other)
    exchange.start()
    half_sums(c, gown)
    exchange.wait_recv()

    scale = 1.0 / math.sqrt(HEAD_DIM)
    by_column = (((1,), (1,)), ((), ()))
    edge_row = lax.broadcasted_iota(jnp.int32, (WINDOW, WINDOW), 0)
    edge_key = lax.broadcasted_iota(jnp.int32, (WINDOW, WINDOW), 1)
    in_window = edge_key > edge_row
    stat_lane = lax.broadcasted_iota(jnp.int32, (WINDOW, HEAD_DIM), 1)
    next_block = block_at(place + 1)
    stat_o[...] = jnp.zeros_like(stat_o)

    def attend_edge(head, carry):
        cols = columns(head)
        queries = edge_q[:, cols]
        keys, values = (ref[pl.ds(ROWS - WINDOW, WINDOW), cols] for ref in (kl, vl))
        stats = stat_o[...]
        for sub in range(HS // HEAD_DIM):
            part = slice(sub * HEAD_DIM, (sub + 1) * HEAD_DIM)
            scores = lax.dot_general(queries[:, part], keys[:, part], by_column, preferred_element_type=F32) * scale
            masked = jnp.where(in_window, scores, -1e30)
            maximum = jnp.max(masked, axis=1, keepdims=True)
            weights = jnp.where(in_window, jnp.exp(masked - maximum), 0.0)
            totals = jnp.sum(weights, axis=1, keepdims=True)
            edge_o[head, :, part] = jnp.dot(weights.astype(BF16), values[:, part], preferred_element_type=F32).astype(BF16)
            lane = head * (HS // HEAD_DIM) + sub
            stats = jnp.where(stat_lane == lane, maximum, jnp.where(stat_lane == lane + 32, totals, stats))
        stat_o[...] = stats
        return carry

    at_row = lax.broadcasted_iota(jnp.int32, (ROWS, ROWS), 0)
    at_key = lax.broadcasted_iota(jnp.int32, (ROWS, ROWS), 1)
    allowed = (at_key > at_row - WINDOW) & (at_key <= at_row)

    def attend(head):
        cols = columns(head)
        queries, keys, values = ql[:, cols], kl[:, cols], vl[:, cols]
        stats = jnp.zeros((WINDOW, HEAD_DIM), F32)
        for sub in range(HS // HEAD_DIM):
            part = slice(sub * HEAD_DIM, (sub + 1) * HEAD_DIM)
            scores = lax.dot_general(queries[:, part], keys[:, part], by_column, preferred_element_type=F32) * scale
            masked = jnp.where(allowed, scores, -1e30)
            maximum = jnp.max(masked, axis=1, keepdims=True)
            weights = jnp.where(allowed, jnp.exp(masked - maximum), 0.0)
            totals = jnp.sum(weights, axis=1, keepdims=True)
            mixed = jnp.dot(weights.astype(BF16), values[:, part], preferred_element_type=F32)
            stats = jnp.where(
                stat_lane == sub, maximum[:WINDOW], jnp.where(stat_lane == sub + 4, totals[:WINDOW], stats)
            )
            att[head, :WINDOW, part] = mixed[:WINDOW]
            att[head, WINDOW:, part] = mixed[WINDOW:] / totals[WINDOW:]
        stat_own[head] = stats

    def merge(head, carry):
        stats, own = stat_in[...], stat_own[head]
        for sub in range(HS // HEAD_DIM):
            part = slice(sub * HEAD_DIM, (sub + 1) * HEAD_DIM)
            lane = head * (HS // HEAD_DIM) + sub
            edge_max, edge_total = (
                jnp.sum(jnp.where(stat_lane == at, stats, 0.0), axis=1, keepdims=True) for at in (lane, lane + 32)
            )
            edge_max = jnp.where(place == 0, -1e30, edge_max)
            maximum, totals = own[:, sub : sub + 1], own[:, sub + 4 : sub + 5]
            both_max = jnp.maximum(maximum, edge_max)
            here, before = jnp.exp(maximum - both_max), jnp.exp(edge_max - both_max)
            first = att[head, :WINDOW, part] * here + edge_in[head, :, part].astype(F32) * before
            att[head, :WINDOW, part] = first / (totals * here + edge_total * before)
        return carry

    def near_sums(i, carry):
        step = lax.rem(i + 1, NZ)
        to = lax.rem(line + step, NZ)
        rows = pl.ds(pl.multiple_of(to * 64, 64), 64)
        gb[pl.ds(to * NX, NX)] = (gown[rows, :] + gex[rows, :].astype(F32)).astype(BF16).reshape(NX, 16, 3 * HS // 2)
        for move in range(1, NX):
            block = gb.at[to * NX + lax.rem(x + move, NX)]
            remote(block, near.at[to * NX + x], nsend, nrecv.at[step], near_mate(move)).start()
        return carry

    lax.fori_loop(0, NZ, near_sums, 0)
    for way in range(OWN):
        remote(q_hbm.at[:, columns(head_of(way))], qb.at[way], qsend, qrecv.at[way], there(way)).start()

    def far_sums(i, carry):
        attend(i)
        step = lax.rem(i + 1, NZ)
        to = lax.rem(line + step, NZ)
        three = near.at[pl.ds(0, NX - 1)]
        remote(three, three, nsend, nrecv.at[step], other).wait_recv()
        near[to * NX + x] = gb[to * NX + x]
        part_sum[to] = jnp.sum(near[pl.ds(to * NX, NX)].astype(F32), axis=0).astype(BF16)

        @pl.when(step > 0)
        def _():
            remote(part_sum.at[to], far.at[line], fsend, frecv, far_mate(step)).start()

        return carry

    lax.fori_loop(0, NZ, far_sums, 0)
    far[line] = part_sum[line]

    seven = far.at[pl.ds(0, NZ - 1)]
    remote(seven, seven, fsend, frecv, other).wait_recv()
    agb[c, spot] = jnp.sum(far[...].astype(F32), axis=0).astype(BF16)
    far_sends(agb, atsend, atrecv)
    near_sends(agb, atsend, atrecv, assend, asrecv)
    for way in range(OWN):
        remote(qb.at[way], qb.at[way], qsend, qrecv.at[way], other).wait_recv()
        qb[way] = normed(qb[way])
    remote(edge_q, edge_q, hqsend, hqrecv, other).wait_recv()
    cross_sends(agb, assend, asrecv, afsend, afrecv, attend_edge)
    remote(edge_o, edge_in, hosend, horecv, next_block).start()
    remote(stat_o, stat_in, hssend, hsrecv, next_block).start()
    crossed(agb, afsend, afrecv)

    def squares(i, total):
        for half in range(2):
            part = agb[half, pl.ds(i * NX, NX)].astype(F32).reshape(64, 3 * HS // 2)
            total = total + jnp.sum(part * part, axis=0, keepdims=True)
        return total

    square_sum = jnp.sum(lax.fori_loop(0, NZ, squares, jnp.zeros((1, 3 * HS // 2), F32)), axis=1, keepdims=True)
    step = STEP_SIZE * lax.rsqrt(square_sum * (1.0 / (3 * HS * HS)) + NORM_EPS)

    def renorm(i, carry):
        rows = pl.ds(pl.multiple_of(i * 64, 64), 64)
        low = agb[0, pl.ds(i * NX, NX)].astype(F32).reshape(64, 3 * HS // 2)
        high = agb[1, pl.ds(i * NX, NX)].astype(F32).reshape(64, 3 * HS // 2)
        for which in range(3):
            part = slice(which * HS // 2, (which + 1) * HS // 2)
            grads = jnp.concatenate([low[:, part], high[:, part]], 1)
            previous = wfull[rows, which * HS : (which + 1) * HS].astype(F32)
            stepped = previous - step * grads
            factor = jnp.sqrt(jnp.mean(previous * previous, axis=-1, keepdims=True)) * lax.rsqrt(
                jnp.mean(stepped * stepped, axis=-1, keepdims=True) + NORM_EPS
            )
            wnew[rows, which * HS : (which + 1) * HS] = (stepped * factor).astype(BF16)
        return carry

    lax.fori_loop(0, NZ, renorm, 0)

    for pair in range(4):
        queries = qb[2 * pair : 2 * pair + 2].reshape(2 * ROWS, HS)
        gate = jnp.dot(queries, wnew[:, :HS], preferred_element_type=F32)
        up = jnp.dot(queries, wnew[:, HS : 2 * HS], preferred_element_type=F32)
        hidden = (gate * jax.nn.sigmoid(gate) * up).astype(BF16)
        result = jnp.dot(hidden, wnew[:, 2 * HS :], preferred_element_type=F32)
        fo[2 * pair : 2 * pair + 2] = result.astype(BF16).reshape(2, ROWS, HS)
        for way in (2 * pair, 2 * pair + 1):
            if way < OWN:
                remote(fo.at[way], ret.at[way], osend, orecv.at[way], there(way, -1)).start()
    remote(edge_in, edge_in, hosend, horecv, other).wait_recv()
    remote(stat_in, stat_in, hssend, hsrecv, other).wait_recv()
    lax.fori_loop(0, HEADS, merge, 0)
    ret[OWN] = fo[OWN]
    for way in (OWN, *range(OWN)):
        if way < OWN:
            remote(ret.at[way], ret.at[way], osend, orecv.at[way], other).wait_recv()
        head = head_of(way)
        out_ref[:, columns(head)] = (att[head] + ret[way].astype(F32)).astype(BF16)

    for buffer, sem in ((kb, ksend), (vb, vsend), (qb, qsend), (ret, osend)):
        sent = buffer.at[pl.ds(0, OWN)]
        remote(sent, sent, sem, orecv.at[0], other).wait_send()
    for buffer, sem in ((edge_q, hqsend), (edge_in, hosend), (stat_in, hssend)):
        remote(buffer, buffer, sem, orecv.at[0], other).wait_send()
    exchange.wait_send()
    for buffer, sem in ((near, nsend), (wrecv.at[0], wssend), (agb.at[0], assend)):
        sent = buffer.at[pl.ds(0, NZ * (NX - 1))]
        remote(sent, sent, sem, orecv.at[0], other).wait_send()
    for sem in (fsend, wtsend, atsend):
        remote(seven, seven, sem, orecv.at[0], other).wait_send()

    @pl.when(jnp.logical_not(is_self))
    def _():
        remote(wpack, wpack, wcsend, orecv.at[0], other).wait_send()

    for buffer, sem in ((wrecv.at[0], wfsend), (agb.at[0], afsend)):
        remote(buffer, buffer, sem, orecv.at[0], other).wait_send()


def shards(queries, key_rows, value_rows, step_rates, w_gate, w_up, w_down):
    hbm = pl.BlockSpec(memory_space=pl.ANY)
    vmem = pl.BlockSpec(memory_space=pltpu.VMEM)
    wide = 3 * HS // 2
    blocks = pltpu.VMEM((8, ROWS, HS), BF16)
    dma = pltpu.SemaphoreType.DMA
    return pl.pallas_call(
        fast_kernel,
        out_shape=jax.ShapeDtypeStruct((ROWS, D), BF16),
        in_specs=[hbm, hbm, hbm, vmem, vmem, vmem, vmem],
        out_specs=vmem,
        scratch_shapes=[
            pltpu.VMEM((ROWS, D), BF16),
            pltpu.VMEM((ROWS, D), BF16),
            pltpu.VMEM((ROWS, D), BF16),
            blocks,
            pltpu.VMEM((WINDOW, D), BF16),
            pltpu.VMEM((8, WINDOW, HS), BF16),
            pltpu.VMEM((8, WINDOW, HS), BF16),
            pltpu.VMEM((WINDOW, HEAD_DIM), F32),
            pltpu.VMEM((WINDOW, HEAD_DIM), F32),
            pltpu.VMEM((8, WINDOW, HEAD_DIM), F32),
            blocks,
            blocks,
            blocks,
            pltpu.VMEM((16, wide), BF16),
            pltpu.VMEM((2, NZ * NX, 16, wide), BF16),
            pltpu.VMEM((HS, 3 * HS), BF16),
            pltpu.VMEM((2, 8, ROWS, HS), BF16),
            blocks,
            pltpu.VMEM((HS, wide), F32),
            pltpu.VMEM((HS, wide), BF16),
            pltpu.VMEM((HS, wide), BF16),
            pltpu.VMEM((NZ * NX, 16, wide), BF16),
            pltpu.VMEM((NZ * NX, 16, wide), BF16),
            pltpu.VMEM((NZ, 16, wide), BF16),
            pltpu.VMEM((NZ, 16, wide), BF16),
            pltpu.VMEM((2, NZ * NX, 16, wide), BF16),
            pltpu.VMEM((HS, 3 * HS), BF16),
            blocks,
            blocks,
            pltpu.VMEM((8, ROWS, HS), F32),
            dma((3,)),
            dma, dma, dma, dma((NZ,)), dma, dma((NZ,)), dma, dma,
            dma, dma((OWN,)), dma, dma((OWN,)), dma, dma((OWN,)),
            dma, dma, dma, dma, dma, dma,
            dma, dma,
            dma, dma((NZ,)), dma, dma,
            dma, dma((NZ,)), dma, dma((NZ,)), dma, dma,
            dma, dma((OWN,)),
        ],
        compiler_params=pltpu.CompilerParams(collective_id=0, has_side_effects=True, vmem_limit_bytes=56 * 1024 * 1024),
    )(queries, key_rows, value_rows, jnp.transpose(step_rates), *(w.reshape(8, HS) for w in (w_gate, w_up, w_down)))


def solution(mesh):
    torus = Mesh(mesh.devices.reshape(NZ, 2, NX, 4, 2), AXES)
    seq = ("z", "yl", "x")
    head = ("yh", "c")
    return jax.shard_map(
        shards,
        mesh=torus,
        in_specs=(
            P((*seq, *head), None),
            P((*seq, *head), None),
            P((*seq, *head), None),
            P((*seq, *head), None),
            P(seq, head, None),
            P(seq, head, None),
            P(seq, head, None),
        ),
        out_specs=P((*seq, *head), None),
        check_vma=False,
    )
```
